32 devices in a mesh: group: 4 (over y, x), member: 8 (over z, core).
Axes of the slice: x: 2, y: 2, z: 4, core: 2. Of those that a mesh axis runs over, the one named last changes fastest.
Arguments:
- a_band: bfloat16 [6144, 3, 64, 64], P(('group', 'member')), as said below
- p_tent: bfloat16 [6144, 6, 64], P(('group', 'member')), may hold values from -0.8984375 to 0.8984375
- new_owner: int32 [6144], P(('group', 'member')), may hold values from 0 to 7, as said below
Outputs:
- p_smooth: bfloat16 [6144, 3, 6, 64], P(('group', 'member'))
- coarse: float32 [6144, 252], P(('group', 'member'))
The draws below stay inside these ranges and needn't reach their ends.
Inputs may be any that keep to these rules, and one draw needn't show every extreme that they name: `new_owner`: within each group, every device sends between 1 and 48 of its block rows to every member of its group, exactly 48 to at least one member, and every member receives exactly 192 block rows. a_band[n, 1, i, i] lies between 2 and 6.
All inputs are finite; a program needn't handle non-finite values.
Results may differ from the reference program's by a relative error of at most 0.0027.
The reference program's roundings to bfloat16 on the way (of `ap`) count: a program that leaves them out, or rounds other values in their place, can miss the bound.
Values may be sent and summed in bfloat16 or wider, within the bound.
A program may use at most 128 MiB of HBM per device.

```python
import jax
import jax.numpy as jnp

TILE = 64
MODES = 6
BR_DEV = 192
CAP = 48
BLOCKS = 6144
N_MEMBER = 8


def draw_a_band(key, part):
    key_one, key_two = jax.random.split(key)
    values = jax.random.normal(key_one, (BLOCKS, 3, TILE, TILE), jnp.float32) * (3 * TILE) ** (-0.5)
    diag = jnp.exp(jax.random.uniform(key_two, (BLOCKS, 3, TILE, TILE), jnp.float32, jnp.log(2.0), jnp.log(6.0)))
    rows = jnp.arange(TILE)[:, None] == jnp.arange(TILE)[None, :]
    center = (jnp.arange(3) == 1)[:, None, None]
    mask = jnp.logical_and(rows[None, :, :], center)[None]
    return jnp.where(mask, diag, values).astype(jnp.bfloat16)


def draw_new_owner(key, part):
    groups = BLOCKS // (BR_DEV * N_MEMBER)
    units = (N_MEMBER - 1) * (CAP - 1)
    extra_total = BR_DEV - N_MEMBER - (CAP - 1)

    def one_group(group_key):
        key_max, key_units, key_src = jax.random.split(group_key, 3)
        heavy = jax.random.randint(key_max, (), 0, N_MEMBER)
        chosen = (jax.random.permutation(key_units, units) < extra_total).astype(jnp.int32)
        extra = chosen.reshape(N_MEMBER - 1, CAP - 1).sum(1)
        bucket = jnp.arange(N_MEMBER - 1, dtype=jnp.int32)
        target = bucket + (bucket >= heavy).astype(jnp.int32)
        counts = jnp.ones((N_MEMBER,), jnp.int32).at[target].add(extra).at[heavy].set(CAP)
        offsets = jnp.repeat(jnp.arange(N_MEMBER, dtype=jnp.int32), counts, total_repeat_length=BR_DEV)

        def one_source(src_key, source):
            order = jax.random.permutation(src_key, BR_DEV)
            return (source + offsets[order]) % N_MEMBER
        src_keys = jax.random.split(key_src, N_MEMBER)
        return jax.vmap(one_source)(src_keys, jnp.arange(N_MEMBER, dtype=jnp.int32)).reshape(-1)
    group_keys = jax.random.split(key, groups)
    return jax.vmap(one_group)(group_keys).reshape(-1).astype(jnp.int32)


def steps_of(stream_key, shape, shards, least, top_value):
    factor_of, own = 1.0, jax.random.fold_in(stream_key, 6)
    for dim, shards_of in shards:
        heights = jnp.exp(jax.random.uniform(jax.random.fold_in(own, dim), (shards_of,), jnp.float32, least / len(shards), top_value / len(shards)))
        factor_of = factor_of * jnp.repeat(heights, shape[dim] // shards_of).reshape([-1 if axis == dim else 1 for axis in range(len(shape))])
    return factor_of


def noise(stream_key, dims, spread, most, pieces=(), kind=jnp.bfloat16):
    array = spread * jax.random.normal(stream_key, dims, jnp.float32)
    if pieces:
        array = array * steps_of(stream_key, dims, pieces, -0.22, 0.18)
    return jnp.clip(array, -most, most).astype(kind)


def setup_inputs(seed: int = 0) -> dict:
    splits = jax.random.split(jax.random.key(seed), 4)
    return {
        "a_band": draw_a_band(jax.random.fold_in(splits[3], 71), 0),
        "p_tent": noise(splits[1], (BLOCKS, MODES, TILE), 0.15, 0.8984375, ((0, 32),)),
        "new_owner": draw_new_owner(jax.random.fold_in(splits[3], 71), 0),
    }


def reference(a_band, p_tent, new_owner):
    nb = a_band.shape[0]
    old_dev = jnp.arange(nb, dtype=jnp.int32) // BR_DEV
    key = (old_dev // N_MEMBER) * N_MEMBER + new_owner.astype(jnp.int32)
    order = jnp.argsort(key, stable=True)
    a_new = a_band[order]
    p_new = p_tent[order]
    dinv = 1.0 / jnp.diagonal(a_new[:, 1], axis1=1, axis2=2).astype(jnp.float32)
    p_rim = jnp.pad(p_new, ((1, 1), (0, 0), (0, 0))).astype(jnp.float32)
    p_self = p_new.astype(jnp.float32)
    tiles = []
    for k in range(3):
        prod = jnp.einsum("nij,ncj->nci", a_new[:, k].astype(jnp.float32), p_rim[k:k + nb])
        base = p_self if k == 1 else jnp.zeros_like(p_self)
        tiles.append(base - 0.6 * dinv[:, None, :] * prod)
    p_smooth = jnp.stack(tiles, 1).astype(jnp.bfloat16)
    s_rim = jnp.pad(p_smooth, ((1, 1), (0, 0), (0, 0), (0, 0))).astype(jnp.float32)
    ap = jnp.zeros((nb, 5, MODES, TILE), jnp.float32)
    for k in range(3):
        prod = jnp.einsum("nij,ntcj->ntci", a_new[:, k].astype(jnp.float32), s_rim[k:k + nb])
        ap = ap + jnp.pad(prod, ((0, 0), (k, 2 - k), (0, 0), (0, 0)))
    ap = ap.astype(jnp.bfloat16)
    both = jnp.concatenate([p_smooth, ap], 1)
    b_rim = jnp.pad(both, ((1, 1), (0, 0), (0, 0), (0, 0))).astype(jnp.float32)
    coarse = jnp.zeros((nb, 7, MODES, MODES), jnp.float32)
    for dn in (-1, 0, 1):
        near = b_rim[1 + dn:1 + dn + nb]
        term = jnp.einsum("nci,nedi->necd", near[:, 1 - dn], near[:, 3:8])
        coarse = coarse + jnp.pad(term, ((0, 0), (1 + dn, 1 - dn), (0, 0), (0, 0)))
    return p_smooth, coarse.reshape(nb, 7 * MODES * MODES)
```

```python
import functools

import jax
import jax.numpy as jnp
from jax import lax
from jax.experimental import pallas as pl
from jax.experimental.pallas import tpu as pltpu
from jax.sharding import PartitionSpec as P

HALO = 3
LANES = 128
MESH = pl.DeviceIdType.MESH


def exchange_kernel(members, slots, send_ref, recv_ref, send_sem, recv_sem, own_sem):
    me = lax.axis_index("member")
    barrier = pltpu.get_barrier_semaphore()

    def greet(o, carry):
        pl.semaphore_signal(
            barrier, inc=1, device_id={"member": lax.rem(me + o, members)}, device_id_type=MESH
        )
        return carry

    lax.fori_loop(1, members, greet, 0)
    pl.semaphore_wait(barrier, members - 1)

    def copy(o):
        other = lax.rem(me + o, members)
        return pltpu.make_async_remote_copy(
            src_ref=send_ref.at[pl.ds(pl.multiple_of(other * slots, slots), slots)],
            dst_ref=recv_ref.at[pl.ds(pl.multiple_of(me * slots, slots), slots)],
            send_sem=send_sem.at[o],
            recv_sem=recv_sem.at[o],
            device_id={"member": other},
            device_id_type=MESH,
        )

    def start(o, carry):
        copy(o).start()
        return carry

    def finish(o, carry):
        copy(o).wait()
        return carry

    lax.fori_loop(1, members, start, 0)
    mine = pl.ds(pl.multiple_of(me * slots, slots), slots)
    own = pltpu.make_async_copy(send_ref.at[mine], recv_ref.at[mine], own_sem)
    own.start()
    own.wait()
    lax.fori_loop(1, members, finish, 0)


def exchange(send, members, slots):
    width = send.shape[1]
    return pl.pallas_call(
        functools.partial(exchange_kernel, members, slots),
        out_shape=jax.ShapeDtypeStruct((members * slots + 16, width), send.dtype),
        in_specs=[pl.BlockSpec(memory_space=pl.ANY)],
        out_specs=pl.BlockSpec(memory_space=pl.ANY),
        scratch_shapes=[
            pltpu.SemaphoreType.DMA((members,)),
            pltpu.SemaphoreType.DMA((members,)),
            pltpu.SemaphoreType.DMA,
        ],
        compiler_params=pltpu.CompilerParams(collective_id=0, has_side_effects=True),
        name="exchange_rows",
    )(send)


def shifted(x, k):
    width = x.shape[-1]
    if k == 0:
        return pltpu.roll(x, 1, axis=x.ndim - 1)
    if k == 2:
        return pltpu.roll(x, width - 1, axis=x.ndim - 1)
    return x


def setup_kernel(a_ref, p_ref, dg_ref, s_ref, co_ref, p3, s3, ap3, dinv):
    modes, tile, width = p_ref.shape
    f32 = jnp.float32
    half = tile // 2
    parts = [(i, l) for l in range(width // LANES) for i in range(2)]
    diag = dg_ref[...]
    dinv[...] = jnp.where(diag > 1.0, 1.0 / jnp.where(diag > 1.0, diag, 1.0), 0.0)
    for c in range(modes):
        own = p_ref[c].astype(f32)
        for k in range(3):
            p3[k, c] = shifted(own, k)

    def product(ks, rows, i0, l0):
        lanes = pl.ds(l0, LANES)

        def body(j8, accs):
            accs = list(accs)
            j0 = pl.multiple_of(j8 * 8, 8)
            for k in ks:
                vecs = [ref[pl.ds(j0, 8), lanes] for ref in rows(k)]
                for jj in range(8):
                    a = a_ref[k, j0 + jj, pl.ds(i0, half), lanes].astype(f32)
                    for c in range(modes):
                        accs[c] = accs[c] + a * vecs[c][jj : jj + 1]
            return tuple(accs)

        zero = jnp.zeros((half, LANES), f32)
        return lax.fori_loop(0, tile // 8, body, (zero,) * modes)

    def each_part(fn):
        def body(q, carry):
            fn(
                pl.multiple_of((q % 2) * half, half),
                pl.multiple_of((q // 2) * LANES, LANES),
            )
            return carry

        lax.fori_loop(0, len(parts), body, 0)

    for k in range(3):

        def smooth(i0, l0, k=k):
            accs = product([k], lambda k: [p3.at[k, c] for c in range(modes)], i0, l0)
            inv = 0.6 * dinv[pl.ds(i0, half), pl.ds(l0, LANES)]
            for c in range(modes):
                value = -inv * accs[c]
                if k == 1:
                    value = p3[1, c, pl.ds(i0, half), pl.ds(l0, LANES)] + value
                value = value.astype(jnp.bfloat16)
                s_ref[k, c, pl.ds(i0, half), pl.ds(l0, LANES)] = value
                s3[1, k, c, pl.ds(i0, half), pl.ds(l0, LANES)] = value.astype(f32)

        each_part(smooth)

    def spread_s(q, carry):
        t, c = q // modes, q % modes
        own = s3[1, t, c]
        s3[0, t, c] = shifted(own, 0)
        s3[2, t, c] = shifted(own, 2)
        return carry

    lax.fori_loop(0, 3 * modes, spread_s, 0)

    for e in range(5):

        def prod(i0, l0, e=e):
            ks = [k for k in range(3) if 0 <= e - k <= 2]
            accs = product(ks, lambda k: [s3.at[k, e - k, c] for c in range(modes)], i0, l0)
            for c in range(modes):
                ap3[1, e, c, pl.ds(i0, half), pl.ds(l0, LANES)] = (
                    accs[c].astype(jnp.bfloat16).astype(f32)
                )

        each_part(prod)

    def spread_ap(q, carry):
        e, c = q // modes, q % modes
        own = ap3[1, e, c]
        ap3[0, e, c] = shifted(own, 0)
        ap3[2, e, c] = shifted(own, 2)
        return carry

    lax.fori_loop(0, 5 * modes, spread_ap, 0)

    for f in range(7):

        def coarse(q, carry, f=f):
            c, l0 = q // (width // LANES), pl.multiple_of((q % (width // LANES)) * LANES, LANES)
            lanes = pl.ds(l0, LANES)
            sums = [None] * modes
            for dn in (-1, 0, 1):
                e = f - 1 - dn
                if not 0 <= e <= 4:
                    continue
                s = s3[dn + 1, 1 - dn, c, :, lanes]
                for d in range(modes):
                    term = s * ap3[dn + 1, e, d, :, lanes]
                    term = jnp.sum(term.reshape(tile // 8, 8, LANES), axis=0)
                    sums[d] = term if sums[d] is None else sums[d] + term
            for d in range(modes):
                co_ref[f, c, d : d + 1, lanes] = jnp.sum(sums[d], axis=0, keepdims=True)
            return carry

        lax.fori_loop(0, modes * (width // LANES), coarse, 0)


def setup(a, p, diag):
    modes, tile, width = p.shape
    f32 = jnp.float32
    return pl.pallas_call(
        setup_kernel,
        out_shape=(
            jax.ShapeDtypeStruct((3, modes, tile, width), jnp.bfloat16),
            jax.ShapeDtypeStruct((7, modes, modes, width), f32),
        ),
        in_specs=[pl.BlockSpec(memory_space=pltpu.VMEM)] * 3,
        out_specs=(pl.BlockSpec(memory_space=pltpu.VMEM),) * 2,
        scratch_shapes=[
            pltpu.VMEM((3, modes, tile, width), f32),
            pltpu.VMEM((3, 3, modes, tile, width), f32),
            pltpu.VMEM((3, 5, modes, tile, width), f32),
            pltpu.VMEM((tile, width), f32),
        ],
        compiler_params=pltpu.CompilerParams(vmem_limit_bytes=56 * 1024 * 1024),
        name="coarse_setup",
    )(a, p, diag)


def per_device(a_band, p_tent, new_owner):
    members = lax.axis_size("member")
    me = lax.axis_index("member")
    rows, _, tile, _ = a_band.shape
    modes = p_tent.shape[1]
    cap = 2 * rows // members
    slots = -(-cap // 16) * 16
    bf16, i32 = jnp.bfloat16, jnp.int32
    size = 3 * tile * tile
    width = -(-(rows + 2 * HALO) // LANES) * LANES

    onehot = (new_owner[None, :] == jnp.arange(members, dtype=i32)[:, None]).astype(i32)
    earlier = (jnp.arange(rows)[:, None] < jnp.arange(rows)[None, :]).astype(jnp.float32)
    before = jnp.dot(onehot.astype(jnp.float32), earlier).astype(i32)
    place = jnp.sum(before * onehot, 0)
    counts = jnp.sum(onehot, 1)
    got = lax.all_gather(counts, "member")[:, me]

    flat_slot = new_owner * slots + place
    pick = (jnp.arange(members * slots, dtype=i32)[:, None] == flat_slot[None, :]).astype(bf16)
    dense = jnp.concatenate(
        [
            a_band.transpose(1, 3, 2, 0).reshape(size, rows),
            p_tent.transpose(1, 2, 0).reshape(modes * tile, rows),
        ],
        0,
    )
    send = lax.dot_general(
        pick, dense, (((1,), (1,)), ((), ())), preferred_element_type=jnp.float32
    ).astype(bf16)
    recv = exchange(send, members, slots)

    ends = jnp.sum(
        jnp.where(jnp.arange(members)[None, :] <= jnp.arange(members)[:, None], got[None, :], 0), 1
    )
    starts = ends - got
    within = jnp.arange(slots, dtype=i32)
    lands = jnp.where(within[None, :] < got[:, None], starts[:, None] + within[None, :], -width)
    lands = lands.reshape(-1)
    edge = jnp.arange(16, dtype=i32)
    edge_row = jnp.where(edge < HALO, edge, jnp.where(edge < 2 * HALO, rows - 2 * HALO + edge, -1))
    rim_pick = (edge_row[:, None] == lands[None, :]).astype(bf16)
    rim = jnp.dot(
        rim_pick, recv[: members * slots], preferred_element_type=jnp.float32
    ).astype(bf16)
    axes = ("group", "member")
    devices = lax.axis_size("group") * members
    up = [(i, i + 1) for i in range(devices - 1)]
    down = [(i + 1, i) for i in range(devices - 1)]
    from_left = lax.ppermute(rim[HALO : 2 * HALO], axes, up)
    from_right = lax.ppermute(rim[:HALO], axes, down)
    halo = jnp.concatenate(
        [from_left, from_right, jnp.zeros((16 - 2 * HALO, rim.shape[1]), bf16)], 0
    )
    recv = lax.dynamic_update_slice(recv, halo, (members * slots, 0))
    halo_lane = jnp.where(edge < HALO, edge, jnp.where(edge < 2 * HALO, rows + edge, -1))
    lane = jnp.concatenate([lands + HALO, halo_lane])
    place_out = (lane[:, None] == jnp.arange(width, dtype=i32)[None, :]).astype(bf16)
    ext = lax.dot_general(
        recv, place_out, (((0,), (0,)), ((), ())), preferred_element_type=jnp.float32
    ).astype(bf16)
    a = ext[:size].reshape(3, tile, tile, width)
    p = ext[size:].reshape(modes, tile, width)
    eye = jnp.eye(tile, dtype=bf16)[:, :, None]
    diag = jnp.sum((a[1] * eye).astype(jnp.float32), 0)
    s_out, co = setup(a, p, diag)
    p_smooth = s_out[..., HALO : HALO + rows].transpose(3, 0, 1, 2)
    coarse = co[..., HALO : HALO + rows].reshape(7 * modes * modes, rows).T
    return (p_smooth, coarse)


def solution(mesh):
    in_specs = (
        P(("group", "member"), None, None, None),
        P(("group", "member"), None, None),
        P(("group", "member")),
    )
    out_specs = (P(("group", "member"), None, None, None), P(("group", "member"), None))
    return jax.shard_map(
        per_device, mesh=mesh, in_specs=in_specs, out_specs=out_specs, check_vma=False
    )
```

```python
import functools

import jax
import jax.numpy as jnp
from jax import lax
from jax.experimental import pallas as pl
from jax.experimental.pallas import tpu as pltpu
from jax.sharding import PartitionSpec as P

HALO = 3
LANES = 128
MESH = pl.DeviceIdType.MESH


def exchange_kernel(members, slots, spill, send_ref, recv_ref, send_sem, recv_sem, own_sem, *sems):
    me = lax.axis_index("member")
    barrier = pltpu.get_barrier_semaphore()

    def greet(o, carry):
        pl.semaphore_signal(
            barrier, inc=1, device_id={"member": lax.rem(me + o, members)}, device_id_type=MESH
        )
        return carry

    lax.fori_loop(1, members, greet, 0)
    pl.semaphore_wait(barrier, members - 1)

    def block(i):
        return pl.ds(pl.multiple_of(i * slots, 16), slots)

    def copy(o):
        other = lax.rem(me + o, members)
        return pltpu.make_async_remote_copy(
            src_ref=send_ref.at[block(other)],
            dst_ref=recv_ref.at[block(me)],
            send_sem=send_sem.at[o],
            recv_sem=recv_sem.at[o],
            device_id={"member": other},
            device_id_type=MESH,
        )

    def start(o, carry):
        copy(o).start()
        return carry

    def finish(o, carry):
        copy(o).wait()
        return carry

    own = pltpu.make_async_copy(send_ref.at[block(me)], recv_ref.at[block(me)], own_sem.at[0])
    if spill:
        chain_send, chain_recv, twin_send, twin_recv = sems
        chips = members // 2
        chip, core = me // 2, me % 2
        last = pl.ds(members * slots, spill)

        def shelf(origin, side):
            at = members * slots + (origin * 2 + side) * spill
            return recv_ref.at[pl.ds(pl.multiple_of(at, 16), spill)]

        def hop(origin, step, src):
            return pltpu.make_async_remote_copy(
                src_ref=src,
                dst_ref=shelf(origin, core),
                send_sem=chain_send.at[origin, (step + 1) // 2],
                recv_sem=chain_recv.at[origin],
                device_id={"member": lax.rem(me + 2 * step + members, members)},
                device_id_type=MESH,
            )

        def twin(origin, src):
            return pltpu.make_async_remote_copy(
                src_ref=src,
                dst_ref=shelf(origin, core),
                send_sem=twin_send.at[origin],
                recv_sem=twin_recv.at[origin],
                device_id={"member": chip * 2 + 1 - core},
                device_id_type=MESH,
            )

        own_last = pltpu.make_async_copy(send_ref.at[last], shelf(chip, core), own_sem.at[1])

        def has(step):
            return jnp.logical_and(chip + step >= 0, chip + step < chips)

        for step in (1, -1):

            @pl.when(has(step))
            def _():
                hop(chip, step, send_ref.at[last]).start()

        twin(chip, send_ref.at[last]).start()
        own_last.start()
        lax.fori_loop(1, members, start, 0)
        own.start()
        for far in range(1, chips):
            for step in (1, -1):
                origin = chip - step * far

                @pl.when(has(-step * far))
                def _():
                    held = shelf(origin, core)
                    hop(origin, step, held).wait_recv()
                    twin(origin, held).start()

                    @pl.when(has(step))
                    def _():
                        hop(origin, step, held).start()

        own_last.wait()
        twin(chip, send_ref.at[last]).wait_send()
        twin(chip, shelf(chip, 1 - core)).wait_recv()
        for step in (1, -1):

            @pl.when(has(step))
            def _():
                hop(chip, step, send_ref.at[last]).wait_send()

        for far in range(1, chips):
            for step in (1, -1):
                origin = chip - step * far

                @pl.when(has(-step * far))
                def _():
                    held = shelf(origin, core)
                    twin(origin, held).wait_send()
                    pltpu.make_async_remote_copy(
                        src_ref=held,
                        dst_ref=shelf(origin, 1 - core),
                        send_sem=twin_send.at[origin],
                        recv_sem=twin_recv.at[origin],
                        device_id={"member": chip * 2 + 1 - core},
                        device_id_type=MESH,
                    ).wait_recv()

                    @pl.when(has(step))
                    def _():
                        hop(origin, step, held).wait_send()

    else:
        lax.fori_loop(1, members, start, 0)
        own.start()
    own.wait()
    lax.fori_loop(1, members, finish, 0)


def exchange(send, members, slots, spill, total):
    width = send.shape[1]
    dma = pltpu.SemaphoreType.DMA
    sems = [dma((members,)), dma((members,)), dma((2,))]
    if spill:
        chips = members // 2
        sems += [dma((chips, 2)), dma((chips,)), dma((chips,)), dma((chips,))]
    return pl.pallas_call(
        functools.partial(exchange_kernel, members, slots, spill),
        out_shape=jax.ShapeDtypeStruct((total, width), send.dtype),
        in_specs=[pl.BlockSpec(memory_space=pl.ANY)],
        out_specs=pl.BlockSpec(memory_space=pl.ANY),
        scratch_shapes=sems,
        compiler_params=pltpu.CompilerParams(
            collective_id=1 if spill else 0, has_side_effects=True
        ),
        name="exchange_spill" if spill else "exchange_rows",
    )(send)


def shifted(x, k):
    width = x.shape[-1]
    if k == 0:
        return pltpu.roll(x, 1, axis=x.ndim - 1)
    if k == 2:
        return pltpu.roll(x, width - 1, axis=x.ndim - 1)
    return x


def setup_kernel(ext_ref, dg_ref, s_ref, co_ref, p3, s3, ap3, dinv):
    _, modes, tile, width = s_ref.shape
    f32 = jnp.float32
    half = tile // 2
    parts = [(i, l) for l in range(width // LANES) for i in range(2)]
    diag = dg_ref[...]
    dinv[...] = jnp.where(diag > 1.0, 1.0 / jnp.where(diag > 1.0, diag, 1.0), 0.0)
    for c in range(modes):
        own = ext_ref[pl.ds((3 * tile + c) * tile, tile), :].astype(f32)
        for k in range(3):
            p3[k, c] = shifted(own, k)

    def product(ks, rows, i0, l0):
        lanes = pl.ds(l0, LANES)

        def body(j8, accs):
            accs = list(accs)
            j0 = pl.multiple_of(j8 * 8, 8)
            for k in ks:
                vecs = [ref[pl.ds(j0, 8), lanes] for ref in rows(k)]
                for jj in range(8):
                    at = pl.multiple_of((k * tile + j0 + jj) * tile + i0, half)
                    a = ext_ref[pl.ds(at, half), lanes].astype(f32)
                    for c in range(modes):
                        accs[c] = accs[c] + a * vecs[c][jj : jj + 1]
            return tuple(accs)

        zero = jnp.zeros((half, LANES), f32)
        return lax.fori_loop(0, tile // 8, body, (zero,) * modes)

    def each_part(fn):
        def body(q, carry):
            fn(
                pl.multiple_of((q % 2) * half, half),
                pl.multiple_of((q // 2) * LANES, LANES),
            )
            return carry

        lax.fori_loop(0, len(parts), body, 0)

    for k in range(3):

        def smooth(i0, l0, k=k):
            accs = product([k], lambda k: [p3.at[k, c] for c in range(modes)], i0, l0)
            inv = 0.6 * dinv[pl.ds(i0, half), pl.ds(l0, LANES)]
            for c in range(modes):
                value = -inv * accs[c]
                if k == 1:
                    value = p3[1, c, pl.ds(i0, half), pl.ds(l0, LANES)] + value
                value = value.astype(jnp.bfloat16)
                s_ref[k, c, pl.ds(i0, half), pl.ds(l0, LANES)] = value
                s3[1, k, c, pl.ds(i0, half), pl.ds(l0, LANES)] = value.astype(f32)

        each_part(smooth)

    def spread_s(q, carry):
        t, c = q // modes, q % modes
        own = s3[1, t, c]
        s3[0, t, c] = shifted(own, 0)
        s3[2, t, c] = shifted(own, 2)
        return carry

    lax.fori_loop(0, 3 * modes, spread_s, 0)

    for e in range(5):

        def prod(i0, l0, e=e):
            ks = [k for k in range(3) if 0 <= e - k <= 2]
            accs = product(ks, lambda k: [s3.at[k, e - k, c] for c in range(modes)], i0, l0)
            for c in range(modes):
                ap3[1, e, c, pl.ds(i0, half), pl.ds(l0, LANES)] = (
                    accs[c].astype(jnp.bfloat16).astype(f32)
                )

        each_part(prod)

    def spread_ap(q, carry):
        e, c = q // modes, q % modes
        own = ap3[1, e, c]
        ap3[0, e, c] = shifted(own, 0)
        ap3[2, e, c] = shifted(own, 2)
        return carry

    lax.fori_loop(0, 5 * modes, spread_ap, 0)

    for f in range(7):

        def coarse(q, carry, f=f):
            c, l0 = q // (width // LANES), pl.multiple_of((q % (width // LANES)) * LANES, LANES)
            lanes = pl.ds(l0, LANES)
            sums = [None] * modes
            for dn in (-1, 0, 1):
                e = f - 1 - dn
                if not 0 <= e <= 4:
                    continue
                s = s3[dn + 1, 1 - dn, c, :, lanes]
                for d in range(modes):
                    term = s * ap3[dn + 1, e, d, :, lanes]
                    term = jnp.sum(term.reshape(tile // 8, 8, LANES), axis=0)
                    sums[d] = term if sums[d] is None else sums[d] + term
            for d in range(modes):
                co_ref[f, c, d : d + 1, lanes] = jnp.sum(sums[d], axis=0, keepdims=True)
            return carry

        lax.fori_loop(0, modes * (width // LANES), coarse, 0)


def setup(ext, diag, modes, tile):
    width = ext.shape[1]
    f32 = jnp.float32
    return pl.pallas_call(
        setup_kernel,
        out_shape=(
            jax.ShapeDtypeStruct((3, modes, tile, width), jnp.bfloat16),
            jax.ShapeDtypeStruct((7, modes, modes, width), f32),
        ),
        in_specs=[pl.BlockSpec(memory_space=pltpu.VMEM)] * 2,
        out_specs=(pl.BlockSpec(memory_space=pltpu.VMEM),) * 2,
        scratch_shapes=[
            pltpu.VMEM((3, modes, tile, width), f32),
            pltpu.VMEM((3, 3, modes, tile, width), f32),
            pltpu.VMEM((3, 5, modes, tile, width), f32),
            pltpu.VMEM((tile, width), f32),
        ],
        compiler_params=pltpu.CompilerParams(vmem_limit_bytes=56 * 1024 * 1024),
        name="coarse_setup",
    )(ext, diag)


def per_device(a_band, p_tent, new_owner):
    members = lax.axis_size("member")
    groups = lax.axis_size("group")
    me = lax.axis_index("member")
    rows, _, tile, _ = a_band.shape
    modes = p_tent.shape[1]
    cap = 2 * rows // members
    slots = -(-cap // 16) * 16
    bf16, i32 = jnp.bfloat16, jnp.int32
    size = 3 * tile * tile
    width = -(-(rows + 2 * HALO) // LANES) * LANES
    spill = 16 if slots > 32 and members % 2 == 0 else 0
    few = slots - spill
    total = max(members * slots, members * (few + spill))

    onehot = (new_owner[None, :] == jnp.arange(members, dtype=i32)[:, None]).astype(i32)
    earlier = (jnp.arange(rows)[:, None] < jnp.arange(rows)[None, :]).astype(jnp.float32)
    before = jnp.dot(onehot.astype(jnp.float32), earlier).astype(i32)
    place = jnp.sum(before * onehot, 0)
    counts = jnp.sum(onehot, 1)
    axes = ("group", "member")
    every = lax.all_gather(counts, axes)
    table = lax.dynamic_slice_in_dim(every, lax.axis_index("group") * members, members, 0)
    got = lax.dynamic_index_in_dim(table, me, 1, keepdims=False)

    dense = jnp.concatenate(
        [
            a_band.transpose(1, 3, 2, 0).reshape(size, rows),
            p_tent.transpose(1, 2, 0).reshape(modes * tile, rows),
        ],
        0,
    )
    member = jnp.arange(members)
    upto = member[None, :] <= member[:, None]
    starts = jnp.sum(jnp.where(upto, got[None, :], 0), 1) - got

    def sorted_send(flat_slot, count):
        pick = (jnp.arange(count, dtype=i32)[:, None] == flat_slot[None, :]).astype(bf16)
        return lax.dot_general(
            pick, dense, (((1,), (1,)), ((), ())), preferred_element_type=jnp.float32
        ).astype(bf16)

    def direct(_):
        send = sorted_send(new_owner * slots + place, members * slots)
        return exchange(send, members, slots, 0, total + 16)

    def direct_lands():
        within = jnp.arange(slots, dtype=i32)
        lands = jnp.where(within[None, :] < got[:, None], starts[:, None] + within[None, :], -width)
        return jnp.pad(lands.reshape(-1), (0, total - members * slots), constant_values=-width)

    if spill:
        over = jnp.maximum(every - few, 0)
        fits = jnp.max(jnp.sum(over, 1)) <= spill

        def spilled(_):
            mine = jnp.maximum(counts - few, 0)
            first = jnp.sum(jnp.where(upto, mine[None, :], 0), 1) - mine
            base = jnp.sum(first[:, None] * onehot, 0)
            slot = jnp.where(
                place < few, new_owner * few + place, members * few + base + place - few
            )
            send = sorted_send(slot, members * few + spill)
            return exchange(send, members, few, spill, total + 16)

        def spilled_lands():
            within = jnp.arange(few, dtype=i32)
            head = jnp.where(
                within[None, :] < got[:, None], starts[:, None] + within[None, :], -width
            )
            over_group = jnp.maximum(table - few, 0)
            before_me = jnp.sum(jnp.where(member[None, :] < me, over_group, 0), 1)
            at = jnp.arange(spill, dtype=i32)[None, :] - before_me[:, None]
            good = jnp.logical_and(at >= 0, at < jnp.maximum(got - few, 0)[:, None])
            tail = jnp.where(good, starts[:, None] + few + at, -width)
            lands = jnp.concatenate([head.reshape(-1), tail.reshape(-1)])
            return jnp.pad(lands, (0, total - members * (few + spill)), constant_values=-width)

        lands = jnp.where(fits, spilled_lands(), direct_lands())
        recv = lax.cond(fits, spilled, direct, 0)
    else:
        lands = direct_lands()
        recv = direct(0)

    edge = jnp.arange(16, dtype=i32)
    edge_row = jnp.where(edge < HALO, edge, jnp.where(edge < 2 * HALO, rows - 2 * HALO + edge, -1))
    rim_pick = (edge_row[:, None] == lands[None, :]).astype(bf16)
    rim = jnp.dot(rim_pick, recv[:total], preferred_element_type=jnp.float32).astype(bf16)
    devices = groups * members
    up = [(i, i + 1) for i in range(devices - 1)]
    down = [(i + 1, i) for i in range(devices - 1)]
    from_left = lax.ppermute(rim[HALO : 2 * HALO], axes, up)
    from_right = lax.ppermute(rim[:HALO], axes, down)
    halo = jnp.concatenate(
        [from_left, from_right, jnp.zeros((16 - 2 * HALO, rim.shape[1]), bf16)], 0
    )
    recv = lax.dynamic_update_slice(recv, halo, (total, 0))
    halo_lane = jnp.where(edge < HALO, edge, jnp.where(edge < 2 * HALO, rows + edge, -1))
    lane = jnp.concatenate([lands + HALO, halo_lane])
    place_out = (lane[:, None] == jnp.arange(width, dtype=i32)[None, :]).astype(bf16)
    ext = lax.dot_general(
        recv, place_out, (((0,), (0,)), ((), ())), preferred_element_type=jnp.float32
    ).astype(bf16)
    centre = ext[tile * tile : 2 * tile * tile].reshape(tile, tile, width)
    eye = jnp.eye(tile, dtype=bf16)[:, :, None]
    diag = jnp.sum((centre * eye).astype(jnp.float32), 0)
    s_out, co = setup(ext, diag, modes, tile)
    p_smooth = s_out[..., HALO : HALO + rows].transpose(3, 0, 1, 2)
    coarse = co[..., HALO : HALO + rows].reshape(7 * modes * modes, rows).T
    return (p_smooth, coarse)


def solution(mesh):
    in_specs = (
        P(("group", "member"), None, None, None),
        P(("group", "member"), None, None),
        P(("group", "member")),
    )
    out_specs = (P(("group", "member"), None, None, None), P(("group", "member"), None))
    return jax.shard_map(
        per_device, mesh=mesh, in_specs=in_specs, out_specs=out_specs, check_vma=False
    )
```

```python
import functools

import jax
import jax.numpy as jnp
from jax import lax
from jax.experimental import pallas as pl
from jax.experimental.pallas import tpu as pltpu
from jax.sharding import PartitionSpec as P

HALO = 3
LANES = 128
MESH = pl.DeviceIdType.MESH


def exchange_kernel(members, slots, spill, send_ref, recv_ref, send_sem, recv_sem, own_sem, *sems):
    me = lax.axis_index("member")
    barrier = pltpu.get_barrier_semaphore()

    def greet(o, carry):
        pl.semaphore_signal(
            barrier, inc=1, device_id={"member": lax.rem(me + o, members)}, device_id_type=MESH
        )
        return carry

    lax.fori_loop(1, members, greet, 0)
    pl.semaphore_wait(barrier, members - 1)

    def block(i):
        return pl.ds(pl.multiple_of(i * slots, 16), slots)

    def copy(o):
        other = lax.rem(me + o, members)
        return pltpu.make_async_remote_copy(
            src_ref=send_ref.at[block(other)],
            dst_ref=recv_ref.at[block(me)],
            send_sem=send_sem.at[o],
            recv_sem=recv_sem.at[o],
            device_id={"member": other},
            device_id_type=MESH,
        )

    def start(o, carry):
        copy(o).start()
        return carry

    def finish(o, carry):
        copy(o).wait()
        return carry

    own = pltpu.make_async_copy(send_ref.at[block(me)], recv_ref.at[block(me)], own_sem.at[0])
    if spill:
        chain_send, chain_recv, twin_send, twin_recv = sems
        chips = members // 2
        chip, core = me // 2, me % 2
        last = pl.ds(members * slots, spill)

        def shelf(origin, side):
            at = members * slots + (origin * 2 + side) * spill
            return recv_ref.at[pl.ds(pl.multiple_of(at, 16), spill)]

        def hop(origin, step, src):
            return pltpu.make_async_remote_copy(
                src_ref=src,
                dst_ref=shelf(origin, core),
                send_sem=chain_send.at[origin, (step + 1) // 2],
                recv_sem=chain_recv.at[origin],
                device_id={"member": lax.rem(me + 2 * step + members, members)},
                device_id_type=MESH,
            )

        def twin(origin, src):
            return pltpu.make_async_remote_copy(
                src_ref=src,
                dst_ref=shelf(origin, core),
                send_sem=twin_send.at[origin],
                recv_sem=twin_recv.at[origin],
                device_id={"member": chip * 2 + 1 - core},
                device_id_type=MESH,
            )

        own_last = pltpu.make_async_copy(send_ref.at[last], shelf(chip, core), own_sem.at[1])

        def has(step):
            return jnp.logical_and(chip + step >= 0, chip + step < chips)

        for step in (1, -1):

            @pl.when(has(step))
            def _():
                hop(chip, step, send_ref.at[last]).start()

        def start_far(far):
            for step in (1, -1):

                @pl.when(has(step * far))
                def _():
                    for side in range(2):
                        copy(lax.rem(members + 2 * step * far + side - core, members)).start()

        twin(chip, send_ref.at[last]).start()
        copy(lax.rem(members + 1 - 2 * core, members)).start()
        own_last.start()
        own.start()
        start_far(1)
        for far in range(1, chips):
            for step in (1, -1):
                origin = chip - step * far

                @pl.when(has(-step * far))
                def _():
                    held = shelf(origin, core)
                    hop(origin, step, held).wait_recv()
                    twin(origin, held).start()

                    @pl.when(has(step))
                    def _():
                        hop(origin, step, held).start()

            if far + 1 < chips:
                start_far(far + 1)

        own_last.wait()
        twin(chip, send_ref.at[last]).wait_send()
        twin(chip, shelf(chip, 1 - core)).wait_recv()
        for step in (1, -1):

            @pl.when(has(step))
            def _():
                hop(chip, step, send_ref.at[last]).wait_send()

        for far in range(1, chips):
            for step in (1, -1):
                origin = chip - step * far

                @pl.when(has(-step * far))
                def _():
                    held = shelf(origin, core)
                    twin(origin, held).wait_send()
                    pltpu.make_async_remote_copy(
                        src_ref=held,
                        dst_ref=shelf(origin, 1 - core),
                        send_sem=twin_send.at[origin],
                        recv_sem=twin_recv.at[origin],
                        device_id={"member": chip * 2 + 1 - core},
                        device_id_type=MESH,
                    ).wait_recv()

                    @pl.when(has(step))
                    def _():
                        hop(origin, step, held).wait_send()

    else:
        lax.fori_loop(1, members, start, 0)
        own.start()
    own.wait()
    lax.fori_loop(1, members, finish, 0)


def exchange(send, members, slots, spill, total):
    width = send.shape[1]
    dma = pltpu.SemaphoreType.DMA
    sems = [dma((members,)), dma((members,)), dma((2,))]
    if spill:
        chips = members // 2
        sems += [dma((chips, 2)), dma((chips,)), dma((chips,)), dma((chips,))]
    return pl.pallas_call(
        functools.partial(exchange_kernel, members, slots, spill),
        out_shape=jax.ShapeDtypeStruct((total, width), send.dtype),
        in_specs=[pl.BlockSpec(memory_space=pl.ANY)],
        out_specs=pl.BlockSpec(memory_space=pl.ANY),
        scratch_shapes=sems,
        compiler_params=pltpu.CompilerParams(
            collective_id=1 if spill else 0, has_side_effects=True
        ),
        name="exchange_spill" if spill else "exchange_rows",
    )(send)


def counts_kernel(groups, members, own_ref, all_ref, send_sem, recv_sem):
    devices = groups * members
    flat = lax.axis_index("group") * members + lax.axis_index("member")
    barrier = pltpu.get_barrier_semaphore()

    def target(o):
        other = lax.rem(flat + o, devices)
        return {"group": other // members, "member": lax.rem(other, members)}

    def greet(o, carry):
        pl.semaphore_signal(barrier, inc=1, device_id=target(o), device_id_type=MESH)
        return carry

    lax.fori_loop(1, devices, greet, 0)
    pl.semaphore_wait(barrier, devices - 1)

    def copy(o):
        return pltpu.make_async_remote_copy(
            src_ref=own_ref,
            dst_ref=all_ref.at[flat],
            send_sem=send_sem.at[o],
            recv_sem=recv_sem.at[o],
            device_id=target(o),
            device_id_type=MESH,
        )

    def start(o, carry):
        copy(o).start()
        return carry

    def finish(o, carry):
        copy(o).wait()
        return carry

    lax.fori_loop(1, devices, start, 0)
    all_ref[flat] = own_ref[...]
    lax.fori_loop(1, devices, finish, 0)


def share_counts(counts, groups, members):
    devices = groups * members
    own = jnp.pad(counts, (0, LANES - members))[None, :]
    return pl.pallas_call(
        functools.partial(counts_kernel, groups, members),
        out_shape=jax.ShapeDtypeStruct((devices, 1, LANES), counts.dtype),
        in_specs=[pl.BlockSpec(memory_space=pltpu.VMEM)],
        out_specs=pl.BlockSpec(memory_space=pltpu.VMEM),
        scratch_shapes=[pltpu.SemaphoreType.DMA((devices,))] * 2,
        compiler_params=pltpu.CompilerParams(collective_id=2, has_side_effects=True),
        name="share_counts",
    )(own)[:, 0, :members]


def shifted(x, k):
    width = x.shape[-1]
    if k == 0:
        return pltpu.roll(x, 1, axis=x.ndim - 1)
    if k == 2:
        return pltpu.roll(x, width - 1, axis=x.ndim - 1)
    return x


def setup_kernel(ext_ref, dg_ref, s_ref, co_ref, p3, s3, ap3, dinv):
    _, modes, tile, width = s_ref.shape
    f32 = jnp.float32
    half = tile // 2
    parts = [(i, l) for l in range(width // LANES) for i in range(2)]
    diag = dg_ref[...]
    dinv[...] = jnp.where(diag > 1.0, 1.0 / jnp.where(diag > 1.0, diag, 1.0), 0.0)
    for c in range(modes):
        own = ext_ref[pl.ds((3 * tile + c) * tile, tile), :].astype(f32)
        for k in range(3):
            p3[k, c] = shifted(own, k)

    def product(ks, rows, i0, l0):
        lanes = pl.ds(l0, LANES)

        def body(j8, accs):
            accs = list(accs)
            j0 = pl.multiple_of(j8 * 8, 8)
            for k in ks:
                vecs = [ref[pl.ds(j0, 8), lanes] for ref in rows(k)]
                for jj in range(8):
                    at = pl.multiple_of((k * tile + j0 + jj) * tile + i0, half)
                    a = ext_ref[pl.ds(at, half), lanes].astype(f32)
                    for c in range(modes):
                        accs[c] = accs[c] + a * vecs[c][jj : jj + 1]
            return tuple(accs)

        zero = jnp.zeros((half, LANES), f32)
        return lax.fori_loop(0, tile // 8, body, (zero,) * modes)

    def each_part(fn):
        def body(q, carry):
            fn(
                pl.multiple_of((q % 2) * half, half),
                pl.multiple_of((q // 2) * LANES, LANES),
            )
            return carry

        lax.fori_loop(0, len(parts), body, 0)

    for k in range(3):

        def smooth(i0, l0, k=k):
            accs = product([k], lambda k: [p3.at[k, c] for c in range(modes)], i0, l0)
            inv = 0.6 * dinv[pl.ds(i0, half), pl.ds(l0, LANES)]
            for c in range(modes):
                value = -inv * accs[c]
                if k == 1:
                    value = p3[1, c, pl.ds(i0, half), pl.ds(l0, LANES)] + value
                value = value.astype(jnp.bfloat16)
                s_ref[k, c, pl.ds(i0, half), pl.ds(l0, LANES)] = value
                s3[1, k, c, pl.ds(i0, half), pl.ds(l0, LANES)] = value.astype(f32)

        each_part(smooth)

    def spread_s(q, carry):
        t, c = q // modes, q % modes
        own = s3[1, t, c]
        s3[0, t, c] = shifted(own, 0)
        s3[2, t, c] = shifted(own, 2)
        return carry

    lax.fori_loop(0, 3 * modes, spread_s, 0)

    for e in range(5):

        def prod(i0, l0, e=e):
            ks = [k for k in range(3) if 0 <= e - k <= 2]
            accs = product(ks, lambda k: [s3.at[k, e - k, c] for c in range(modes)], i0, l0)
            for c in range(modes):
                ap3[1, e, c, pl.ds(i0, half), pl.ds(l0, LANES)] = (
                    accs[c].astype(jnp.bfloat16).astype(f32)
                )

        each_part(prod)

    def spread_ap(q, carry):
        e, c = q // modes, q % modes
        own = ap3[1, e, c]
        ap3[0, e, c] = shifted(own, 0)
        ap3[2, e, c] = shifted(own, 2)
        return carry

    lax.fori_loop(0, 5 * modes, spread_ap, 0)

    for f in range(7):

        def coarse(q, carry, f=f):
            c, l0 = q // (width // LANES), pl.multiple_of((q % (width // LANES)) * LANES, LANES)
            lanes = pl.ds(l0, LANES)
            sums = [None] * modes
            for dn in (-1, 0, 1):
                e = f - 1 - dn
                if not 0 <= e <= 4:
                    continue
                s = s3[dn + 1, 1 - dn, c, :, lanes]
                for d in range(modes):
                    term = s * ap3[dn + 1, e, d, :, lanes]
                    term = jnp.sum(term.reshape(tile // 8, 8, LANES), axis=0)
                    sums[d] = term if sums[d] is None else sums[d] + term
            for d in range(modes):
                co_ref[f, c, d : d + 1, lanes] = jnp.sum(sums[d], axis=0, keepdims=True)
            return carry

        lax.fori_loop(0, modes * (width // LANES), coarse, 0)


def setup(ext, diag, modes, tile):
    width = ext.shape[1]
    f32 = jnp.float32
    return pl.pallas_call(
        setup_kernel,
        out_shape=(
            jax.ShapeDtypeStruct((3, modes, tile, width), jnp.bfloat16),
            jax.ShapeDtypeStruct((7, modes, modes, width), f32),
        ),
        in_specs=[pl.BlockSpec(memory_space=pltpu.VMEM)] * 2,
        out_specs=(pl.BlockSpec(memory_space=pltpu.VMEM),) * 2,
        scratch_shapes=[
            pltpu.VMEM((3, modes, tile, width), f32),
            pltpu.VMEM((3, 3, modes, tile, width), f32),
            pltpu.VMEM((3, 5, modes, tile, width), f32),
            pltpu.VMEM((tile, width), f32),
        ],
        compiler_params=pltpu.CompilerParams(vmem_limit_bytes=56 * 1024 * 1024),
        name="coarse_setup",
    )(ext, diag)


def per_device(a_band, p_tent, new_owner):
    members = lax.axis_size("member")
    groups = lax.axis_size("group")
    me = lax.axis_index("member")
    rows, _, tile, _ = a_band.shape
    modes = p_tent.shape[1]
    cap = 2 * rows // members
    slots = -(-cap // 16) * 16
    bf16, i32 = jnp.bfloat16, jnp.int32
    size = 3 * tile * tile
    width = -(-(rows + 2 * HALO) // LANES) * LANES
    spill = 16 if slots > 32 and members % 2 == 0 else 0
    few = slots - spill
    total = max(members * slots, members * (few + spill))

    onehot = (new_owner[None, :] == jnp.arange(members, dtype=i32)[:, None]).astype(i32)
    earlier = (jnp.arange(rows)[:, None] < jnp.arange(rows)[None, :]).astype(jnp.float32)
    before = jnp.dot(onehot.astype(jnp.float32), earlier).astype(i32)
    place = jnp.sum(before * onehot, 0)
    counts = jnp.sum(onehot, 1)
    axes = ("group", "member")
    if spill:
        every = share_counts(counts, groups, members)
        table = lax.dynamic_slice_in_dim(every, lax.axis_index("group") * members, members, 0)
    else:
        table = lax.all_gather(counts, "member")
    got = lax.dynamic_index_in_dim(table, me, 1, keepdims=False)

    dense = jnp.concatenate(
        [
            a_band.transpose(1, 3, 2, 0).reshape(size, rows),
            p_tent.transpose(1, 2, 0).reshape(modes * tile, rows),
        ],
        0,
    )
    member = jnp.arange(members)
    upto = member[None, :] <= member[:, None]
    starts = jnp.sum(jnp.where(upto, got[None, :], 0), 1) - got

    def sorted_send(flat_slot, count):
        pick = (jnp.arange(count, dtype=i32)[:, None] == flat_slot[None, :]).astype(bf16)
        return lax.dot_general(
            pick, dense, (((1,), (1,)), ((), ())), preferred_element_type=jnp.float32
        ).astype(bf16)

    flat_slot = new_owner * slots + place

    def direct(send):
        return exchange(send, members, slots, 0, total + 16)

    def direct_lands():
        within = jnp.arange(slots, dtype=i32)
        lands = jnp.where(within[None, :] < got[:, None], starts[:, None] + within[None, :], -width)
        return jnp.pad(lands.reshape(-1), (0, total - members * slots), constant_values=-width)

    if spill:
        over = jnp.maximum(every - few, 0)
        fits = jnp.max(jnp.sum(over, 1)) <= spill

        mine = jnp.maximum(counts - few, 0)
        first = jnp.sum(jnp.where(upto, mine[None, :], 0), 1) - mine
        base = jnp.sum(first[:, None] * onehot, 0)
        spill_slot = jnp.where(
            place < few, new_owner * few + place, members * few + base + place - few
        )

        def spilled(send):
            return exchange(send, members, few, spill, total + 16)

        def spilled_lands():
            within = jnp.arange(few, dtype=i32)
            head = jnp.where(
                within[None, :] < got[:, None], starts[:, None] + within[None, :], -width
            )
            over_group = jnp.maximum(table - few, 0)
            before_me = jnp.sum(jnp.where(member[None, :] < me, over_group, 0), 1)
            at = jnp.arange(spill, dtype=i32)[None, :] - before_me[:, None]
            good = jnp.logical_and(at >= 0, at < jnp.maximum(got - few, 0)[:, None])
            tail = jnp.where(good, starts[:, None] + few + at, -width)
            lands = jnp.concatenate([head.reshape(-1), tail.reshape(-1)])
            return jnp.pad(lands, (0, total - members * (few + spill)), constant_values=-width)

        lands = jnp.where(fits, spilled_lands(), direct_lands())
        send = sorted_send(jnp.where(fits, spill_slot, flat_slot), members * slots)
        recv = lax.cond(fits, spilled, direct, send)
    else:
        lands = direct_lands()
        recv = direct(sorted_send(flat_slot, members * slots))

    edge = jnp.arange(16, dtype=i32)
    edge_row = jnp.where(edge < HALO, edge, jnp.where(edge < 2 * HALO, rows - 2 * HALO + edge, -1))
    rim_pick = (edge_row[:, None] == lands[None, :]).astype(bf16)
    rim = jnp.dot(rim_pick, recv[:total], preferred_element_type=jnp.float32).astype(bf16)
    devices = groups * members
    up = [(i, i + 1) for i in range(devices - 1)]
    down = [(i + 1, i) for i in range(devices - 1)]
    from_left = lax.ppermute(rim[HALO : 2 * HALO], axes, up)
    from_right = lax.ppermute(rim[:HALO], axes, down)
    halo = jnp.concatenate(
        [from_left, from_right, jnp.zeros((16 - 2 * HALO, rim.shape[1]), bf16)], 0
    )
    recv = lax.dynamic_update_slice(recv, halo, (total, 0))
    halo_lane = jnp.where(edge < HALO, edge, jnp.where(edge < 2 * HALO, rows + edge, -1))
    lane = jnp.concatenate([lands + HALO, halo_lane])
    place_out = (lane[:, None] == jnp.arange(width, dtype=i32)[None, :]).astype(bf16)
    ext = lax.dot_general(
        recv, place_out, (((0,), (0,)), ((), ())), preferred_element_type=jnp.float32
    ).astype(bf16)
    centre = ext[tile * tile : 2 * tile * tile].reshape(tile, tile, width)
    eye = jnp.eye(tile, dtype=bf16)[:, :, None]
    diag = jnp.sum((centre * eye).astype(jnp.float32), 0)
    s_out, co = setup(ext, diag, modes, tile)
    p_smooth = s_out[..., HALO : HALO + rows].transpose(3, 0, 1, 2)
    coarse = co[..., HALO : HALO + rows].reshape(7 * modes * modes, rows).T
    return (p_smooth, coarse)


def solution(mesh):
    in_specs = (
        P(("group", "member"), None, None, None),
        P(("group", "member"), None, None),
        P(("group", "member")),
    )
    out_specs = (P(("group", "member"), None, None, None), P(("group", "member"), None))
    return jax.shard_map(
        per_device, mesh=mesh, in_specs=in_specs, out_specs=out_specs, check_vma=False
    )
```

```python
import functools

import jax
import jax.numpy as jnp
from jax import lax
from jax.experimental import pallas as pl
from jax.experimental.pallas import tpu as pltpu
from jax.sharding import PartitionSpec as P

HALO = 3
LANES = 128
MESH = pl.DeviceIdType.MESH


def exchange_kernel(
    members, slots, spill, step_lanes, pick_ref, a_ref, p_ref, recv_ref, send_ref, blank_ref,
    blank_sem, send_sem, recv_sem, own_sem, *sems
):
    me = lax.axis_index("member")
    barrier = pltpu.get_barrier_semaphore()

    def greet(o, carry):
        pl.semaphore_signal(
            barrier, inc=1, device_id={"member": lax.rem(me + o, members)}, device_id_type=MESH
        )
        return carry

    lax.fori_loop(1, members, greet, 0)
    blank_ref[...] = jnp.zeros_like(blank_ref)
    spare = pl.ds(recv_ref.shape[0] - 16, 16)
    blank = pltpu.make_async_copy(blank_ref, recv_ref.at[spare], blank_sem)
    blank.start()

    steps = a_ref.shape[0] // step_lanes
    cuts = ((0, 4), (4, steps + 1))

    def gathered(rows):
        return lax.dot_general(
            pick_ref[...], rows, (((1,), (1,)), ((), ())), preferred_element_type=jnp.float32
        ).astype(send_ref.dtype)

    def gather(first, end):
        def body(i, carry):
            at = pl.ds(pl.multiple_of(i * step_lanes, step_lanes), step_lanes)
            send_ref[:, at] = gathered(a_ref[at, :])
            return carry

        lax.fori_loop(first, min(end, steps), body, 0)
        if end > steps:
            send_ref[:, steps * step_lanes :] = gathered(p_ref[...])

    def lanes(n):
        return pl.ds(cuts[n][0] * step_lanes, (cuts[n][1] - cuts[n][0]) * step_lanes)

    def block(i):
        return pl.ds(pl.multiple_of(i * slots, 16), slots)

    def copy(n, o):
        other = lax.rem(me + o, members)
        return pltpu.make_async_remote_copy(
            src_ref=send_ref.at[block(other), lanes(n)],
            dst_ref=recv_ref.at[block(me), lanes(n)],
            send_sem=send_sem.at[n, o],
            recv_sem=recv_sem.at[n, o],
            device_id={"member": other},
            device_id_type=MESH,
        )

    def own(n):
        return pltpu.make_async_copy(
            send_ref.at[block(me), lanes(n)], recv_ref.at[block(me), lanes(n)], own_sem.at[n, 0]
        )

    def start_all(n):
        def start(o, carry):
            copy(n, o).start()
            return carry

        lax.fori_loop(1, members, start, 0)
        own(n).start()

    def finish_all(n):
        def finish(o, carry):
            copy(n, o).wait()
            return carry

        own(n).wait()
        lax.fori_loop(1, members, finish, 0)

    if not spill:
        gather(*cuts[0])
        pl.semaphore_wait(barrier, members - 1)
        start_all(0)
        gather(*cuts[1])
        start_all(1)
        finish_all(0)
        finish_all(1)
        blank.wait()
        return

    chain_send, chain_recv, twin_send, twin_recv = sems
    chips = members // 2
    chip, core = me // 2, me % 2

    def last(n):
        return send_ref.at[pl.ds(members * slots, spill), lanes(n)]

    def shelf(n, origin, side):
        at = members * slots + (origin * 2 + side) * spill
        return recv_ref.at[pl.ds(pl.multiple_of(at, 16), spill), lanes(n)]

    def hop(n, origin, step, src):
        return pltpu.make_async_remote_copy(
            src_ref=src,
            dst_ref=shelf(n, origin, core),
            send_sem=chain_send.at[n, origin, (step + 1) // 2],
            recv_sem=chain_recv.at[n, origin],
            device_id={"member": lax.rem(me + 2 * step + members, members)},
            device_id_type=MESH,
        )

    def twin(n, origin, src, side):
        return pltpu.make_async_remote_copy(
            src_ref=src,
            dst_ref=shelf(n, origin, side),
            send_sem=twin_send.at[n, origin],
            recv_sem=twin_recv.at[n, origin],
            device_id={"member": chip * 2 + 1 - core},
            device_id_type=MESH,
        )

    def own_last(n):
        return pltpu.make_async_copy(last(n), shelf(n, chip, core), own_sem.at[n, 1])

    def has(step):
        return jnp.logical_and(chip + step >= 0, chip + step < chips)

    def launch(n):
        for step in (1, -1):

            @pl.when(has(step))
            def _():
                hop(n, chip, step, last(n)).start()

        twin(n, chip, last(n), core).start()
        own_last(n).start()
        start_all(n)

    gather(*cuts[0])
    pl.semaphore_wait(barrier, members - 1)
    launch(0)
    gather(*cuts[1])
    launch(1)
    for n in range(2):
        for far in range(1, chips):
            for step in (1, -1):
                origin = chip - step * far

                @pl.when(has(-step * far))
                def _():
                    held = shelf(n, origin, core)
                    hop(n, origin, step, held).wait_recv()
                    twin(n, origin, held, core).start()

                    @pl.when(has(step))
                    def _():
                        hop(n, origin, step, held).start()

    for n in range(2):
        own_last(n).wait()
        twin(n, chip, last(n), core).wait_send()
        twin(n, chip, last(n), 1 - core).wait_recv()
        for step in (1, -1):

            @pl.when(has(step))
            def _():
                hop(n, chip, step, last(n)).wait_send()

        for far in range(1, chips):
            for step in (1, -1):
                origin = chip - step * far

                @pl.when(has(-step * far))
                def _():
                    held = shelf(n, origin, core)
                    twin(n, origin, held, core).wait_send()
                    twin(n, origin, held, 1 - core).wait_recv()

                    @pl.when(has(step))
                    def _():
                        hop(n, origin, step, held).wait_send()

        finish_all(n)
    blank.wait()


def exchange(pick, a_rows, p_rows, members, slots, spill, total):
    size, step_lanes = a_rows.shape[0], p_rows.shape[0]
    dma = pltpu.SemaphoreType.DMA
    width = size + step_lanes
    sems = [dma((2, members)), dma((2, members)), dma((2, 2))]
    if spill:
        chips = members // 2
        sems += [dma((2, chips, 2)), dma((2, chips)), dma((2, chips)), dma((2, chips))]
    return pl.pallas_call(
        functools.partial(exchange_kernel, members, slots, spill, step_lanes),
        out_shape=jax.ShapeDtypeStruct((total, width), a_rows.dtype),
        in_specs=[pl.BlockSpec(memory_space=pltpu.VMEM)] * 3,
        out_specs=pl.BlockSpec(memory_space=pl.ANY),
        scratch_shapes=[
            pltpu.VMEM((pick.shape[0], width), a_rows.dtype),
            pltpu.VMEM((16, width), a_rows.dtype),
            dma,
        ]
        + sems,
        compiler_params=pltpu.CompilerParams(
            collective_id=1 if spill else 0,
            has_side_effects=True,
            vmem_limit_bytes=44 * 1024 * 1024,
        ),
        name="exchange_spill" if spill else "exchange_rows",
    )(pick, a_rows, p_rows)


def counts_kernel(groups, members, own_ref, all_ref, send_sem, recv_sem):
    devices = groups * members
    flat = lax.axis_index("group") * members + lax.axis_index("member")
    barrier = pltpu.get_barrier_semaphore()

    def target(o):
        other = lax.rem(flat + o, devices)
        return {"group": other // members, "member": lax.rem(other, members)}

    def greet(o, carry):
        pl.semaphore_signal(barrier, inc=1, device_id=target(o), device_id_type=MESH)
        return carry

    lax.fori_loop(1, devices, greet, 0)
    pl.semaphore_wait(barrier, devices - 1)

    def copy(o):
        return pltpu.make_async_remote_copy(
            src_ref=own_ref,
            dst_ref=all_ref.at[flat],
            send_sem=send_sem.at[o],
            recv_sem=recv_sem.at[o],
            device_id=target(o),
            device_id_type=MESH,
        )

    def start(o, carry):
        copy(o).start()
        return carry

    def finish(o, carry):
        copy(o).wait()
        return carry

    lax.fori_loop(1, devices, start, 0)
    all_ref[flat] = own_ref[...]
    lax.fori_loop(1, devices, finish, 0)


def share_counts(counts, groups, members):
    devices = groups * members
    own = jnp.pad(counts, (0, LANES - members))[None, :]
    return pl.pallas_call(
        functools.partial(counts_kernel, groups, members),
        out_shape=jax.ShapeDtypeStruct((devices, 1, LANES), counts.dtype),
        in_specs=[pl.BlockSpec(memory_space=pltpu.VMEM)],
        out_specs=pl.BlockSpec(memory_space=pltpu.VMEM),
        scratch_shapes=[pltpu.SemaphoreType.DMA((devices,))] * 2,
        compiler_params=pltpu.CompilerParams(collective_id=2, has_side_effects=True),
        name="share_counts",
    )(own)[:, 0, :members]


def shifted(x, k):
    width = x.shape[-1]
    if k == 0:
        return pltpu.roll(x, 1, axis=x.ndim - 1)
    if k == 2:
        return pltpu.roll(x, width - 1, axis=x.ndim - 1)
    return x


def setup_kernel(ext_ref, dg_ref, s_ref, co_ref, p3, s3, ap3, dinv):
    _, modes, tile, width = s_ref.shape
    f32 = jnp.float32
    half = tile // 2
    parts = [(i, l) for l in range(width // LANES) for i in range(2)]
    diag = dg_ref[...]
    dinv[...] = jnp.where(diag > 1.0, 1.0 / jnp.where(diag > 1.0, diag, 1.0), 0.0)
    for c in range(modes):
        own = ext_ref[pl.ds((3 * tile + c) * tile, tile), :].astype(f32)
        for k in range(3):
            p3[k, c] = shifted(own, k)

    def product(ks, rows, i0, l0):
        lanes = pl.ds(l0, LANES)

        def body(j8, accs):
            accs = list(accs)
            j0 = pl.multiple_of(j8 * 8, 8)
            for k in ks:
                vecs = [ref[pl.ds(j0, 8), lanes] for ref in rows(k)]
                for jj in range(8):
                    at = pl.multiple_of((k * tile + j0 + jj) * tile + i0, half)
                    a = ext_ref[pl.ds(at, half), lanes].astype(f32)
                    for c in range(modes):
                        accs[c] = accs[c] + a * vecs[c][jj : jj + 1]
            return tuple(accs)

        zero = jnp.zeros((half, LANES), f32)
        return lax.fori_loop(0, tile // 8, body, (zero,) * modes)

    def each_part(fn):
        def body(q, carry):
            fn(
                pl.multiple_of((q % 2) * half, half),
                pl.multiple_of((q // 2) * LANES, LANES),
            )
            return carry

        lax.fori_loop(0, len(parts), body, 0)

    for k in range(3):

        def smooth(i0, l0, k=k):
            accs = product([k], lambda k: [p3.at[k, c] for c in range(modes)], i0, l0)
            inv = 0.6 * dinv[pl.ds(i0, half), pl.ds(l0, LANES)]
            for c in range(modes):
                value = -inv * accs[c]
                if k == 1:
                    value = p3[1, c, pl.ds(i0, half), pl.ds(l0, LANES)] + value
                value = value.astype(jnp.bfloat16)
                s_ref[k, c, pl.ds(i0, half), pl.ds(l0, LANES)] = value
                s3[1, k, c, pl.ds(i0, half), pl.ds(l0, LANES)] = value.astype(f32)

        each_part(smooth)

    def spread_s(q, carry):
        t, c = q // modes, q % modes
        own = s3[1, t, c]
        s3[0, t, c] = shifted(own, 0)
        s3[2, t, c] = shifted(own, 2)
        return carry

    lax.fori_loop(0, 3 * modes, spread_s, 0)

    for e in range(5):

        def prod(i0, l0, e=e):
            ks = [k for k in range(3) if 0 <= e - k <= 2]
            accs = product(ks, lambda k: [s3.at[k, e - k, c] for c in range(modes)], i0, l0)
            for c in range(modes):
                ap3[1, e, c, pl.ds(i0, half), pl.ds(l0, LANES)] = (
                    accs[c].astype(jnp.bfloat16).astype(f32)
                )

        each_part(prod)

    def spread_ap(q, carry):
        e, c = q // modes, q % modes
        own = ap3[1, e, c]
        ap3[0, e, c] = shifted(own, 0)
        ap3[2, e, c] = shifted(own, 2)
        return carry

    lax.fori_loop(0, 5 * modes, spread_ap, 0)

    for f in range(7):

        def coarse(q, carry, f=f):
            c, l0 = q // (width // LANES), pl.multiple_of((q % (width // LANES)) * LANES, LANES)
            lanes = pl.ds(l0, LANES)
            sums = [None] * modes
            for dn in (-1, 0, 1):
                e = f - 1 - dn
                if not 0 <= e <= 4:
                    continue
                s = s3[dn + 1, 1 - dn, c, :, lanes]
                for d in range(modes):
                    term = s * ap3[dn + 1, e, d, :, lanes]
                    term = jnp.sum(term.reshape(tile // 8, 8, LANES), axis=0)
                    sums[d] = term if sums[d] is None else sums[d] + term
            for d in range(modes):
                co_ref[f, c, d : d + 1, lanes] = jnp.sum(sums[d], axis=0, keepdims=True)
            return carry

        lax.fori_loop(0, modes * (width // LANES), coarse, 0)


def setup(ext, diag, modes, tile):
    width = ext.shape[1]
    f32 = jnp.float32
    return pl.pallas_call(
        setup_kernel,
        out_shape=(
            jax.ShapeDtypeStruct((3, modes, tile, width), jnp.bfloat16),
            jax.ShapeDtypeStruct((7, modes, modes, width), f32),
        ),
        in_specs=[pl.BlockSpec(memory_space=pltpu.VMEM)] * 2,
        out_specs=(pl.BlockSpec(memory_space=pltpu.VMEM),) * 2,
        scratch_shapes=[
            pltpu.VMEM((3, modes, tile, width), f32),
            pltpu.VMEM((3, 3, modes, tile, width), f32),
            pltpu.VMEM((3, 5, modes, tile, width), f32),
            pltpu.VMEM((tile, width), f32),
        ],
        compiler_params=pltpu.CompilerParams(vmem_limit_bytes=56 * 1024 * 1024),
        name="coarse_setup",
    )(ext, diag)


def per_device(a_band, p_tent, new_owner):
    members = lax.axis_size("member")
    groups = lax.axis_size("group")
    me = lax.axis_index("member")
    rows, _, tile, _ = a_band.shape
    modes = p_tent.shape[1]
    cap = 2 * rows // members
    slots = -(-cap // 16) * 16
    bf16, i32 = jnp.bfloat16, jnp.int32
    size = 3 * tile * tile
    width = -(-(rows + 2 * HALO) // LANES) * LANES
    spill = 16 if slots > 32 and members % 2 == 0 else 0
    few = slots - spill
    total = max(members * slots, members * (few + spill))

    onehot = (new_owner[None, :] == jnp.arange(members, dtype=i32)[:, None]).astype(i32)
    earlier = (jnp.arange(rows)[:, None] < jnp.arange(rows)[None, :]).astype(jnp.float32)
    before = jnp.dot(onehot.astype(jnp.float32), earlier).astype(i32)
    place = jnp.sum(before * onehot, 0)
    counts = jnp.sum(onehot, 1)
    axes = ("group", "member")
    if spill:
        every = share_counts(counts, groups, members)
        table = lax.dynamic_slice_in_dim(every, lax.axis_index("group") * members, members, 0)
    else:
        table = lax.all_gather(counts, "member")
    got = lax.dynamic_index_in_dim(table, me, 1, keepdims=False)

    a_rows = a_band.transpose(1, 3, 2, 0).reshape(size, rows)
    p_rows = p_tent.transpose(1, 2, 0).reshape(modes * tile, rows)
    member = jnp.arange(members)
    upto = member[None, :] <= member[:, None]
    starts = jnp.sum(jnp.where(upto, got[None, :], 0), 1) - got

    def picked(flat_slot, count):
        return (jnp.arange(count, dtype=i32)[:, None] == flat_slot[None, :]).astype(bf16)

    flat_slot = new_owner * slots + place

    def direct(own_a, own_p):
        pick = picked(flat_slot, members * slots)
        return exchange(pick, own_a, own_p, members, slots, 0, total + 16)

    def direct_lands():
        within = jnp.arange(slots, dtype=i32)
        lands = jnp.where(within[None, :] < got[:, None], starts[:, None] + within[None, :], -width)
        return jnp.pad(lands.reshape(-1), (0, total - members * slots), constant_values=-width)

    if spill:
        over = jnp.maximum(every - few, 0)
        fits = jnp.max(jnp.sum(over, 1)) <= spill

        mine = jnp.maximum(counts - few, 0)
        first = jnp.sum(jnp.where(upto, mine[None, :], 0), 1) - mine
        base = jnp.sum(first[:, None] * onehot, 0)
        spill_slot = jnp.where(
            place < few, new_owner * few + place, members * few + base + place - few
        )

        def spilled(own_a, own_p):
            pick = picked(spill_slot, members * few + spill)
            return exchange(pick, own_a, own_p, members, few, spill, total + 16)

        def spilled_lands():
            within = jnp.arange(few, dtype=i32)
            head = jnp.where(
                within[None, :] < got[:, None], starts[:, None] + within[None, :], -width
            )
            over_group = jnp.maximum(table - few, 0)
            before_me = jnp.sum(jnp.where(member[None, :] < me, over_group, 0), 1)
            at = jnp.arange(spill, dtype=i32)[None, :] - before_me[:, None]
            good = jnp.logical_and(at >= 0, at < jnp.maximum(got - few, 0)[:, None])
            tail = jnp.where(good, starts[:, None] + few + at, -width)
            lands = jnp.concatenate([head.reshape(-1), tail.reshape(-1)])
            return jnp.pad(lands, (0, total - members * (few + spill)), constant_values=-width)

        lands = jnp.where(fits, spilled_lands(), direct_lands())
        recv = lax.cond(fits, spilled, direct, a_rows, p_rows)
    else:
        lands = direct_lands()
        recv = direct(a_rows, p_rows)

    edge = jnp.arange(16, dtype=i32)
    edge_row = jnp.where(edge < HALO, edge, jnp.where(edge < 2 * HALO, rows - 2 * HALO + edge, -1))
    filled = jnp.concatenate([lands, jnp.full((16,), -width, i32)])
    rim_pick = (edge_row[:, None] == filled[None, :]).astype(bf16)
    rim = jnp.dot(rim_pick, recv, preferred_element_type=jnp.float32).astype(bf16)
    devices = groups * members
    up = [(i, i + 1) for i in range(devices - 1)]
    down = [(i + 1, i) for i in range(devices - 1)]
    from_left = lax.ppermute(rim[HALO : 2 * HALO], axes, up)
    from_right = lax.ppermute(rim[:HALO], axes, down)
    halo = jnp.concatenate(
        [from_left, from_right, jnp.zeros((16 - 2 * HALO, rim.shape[1]), bf16)], 0
    )
    recv = lax.dynamic_update_slice(recv, halo, (total, 0))
    halo_lane = jnp.where(edge < HALO, edge, jnp.where(edge < 2 * HALO, rows + edge, -1))
    lane = jnp.concatenate([lands + HALO, halo_lane])
    place_out = (lane[:, None] == jnp.arange(width, dtype=i32)[None, :]).astype(bf16)
    ext = lax.dot_general(
        recv, place_out, (((0,), (0,)), ((), ())), preferred_element_type=jnp.float32
    ).astype(bf16)
    centre = ext[tile * tile : 2 * tile * tile].reshape(tile, tile, width)
    eye = jnp.eye(tile, dtype=bf16)[:, :, None]
    diag = jnp.sum((centre * eye).astype(jnp.float32), 0)
    s_out, co = setup(ext, diag, modes, tile)
    p_smooth = s_out[..., HALO : HALO + rows].transpose(3, 0, 1, 2)
    coarse = co[..., HALO : HALO + rows].reshape(7 * modes * modes, rows).T
    return (p_smooth, coarse)


def solution(mesh):
    in_specs = (
        P(("group", "member"), None, None, None),
        P(("group", "member"), None, None),
        P(("group", "member")),
    )
    out_specs = (P(("group", "member"), None, None, None), P(("group", "member"), None))
    return jax.shard_map(
        per_device, mesh=mesh, in_specs=in_specs, out_specs=out_specs, check_vma=False
    )
```

```python
import functools

import jax
import jax.numpy as jnp
from jax import lax
from jax.experimental import pallas as pl
from jax.experimental.pallas import tpu as pltpu
from jax.sharding import PartitionSpec as P

HALO = 3
LANES = 128
MESH = pl.DeviceIdType.MESH


def exchange_kernel(
    members, slots, spill, step_lanes, pick_ref, a_ref, p_ref, recv_ref, send_ref, blank_ref,
    blank_sem, send_sem, recv_sem, own_sem, *sems
):
    me = lax.axis_index("member")
    barrier = pltpu.get_barrier_semaphore()

    def greet(o, carry):
        pl.semaphore_signal(
            barrier, inc=1, device_id={"member": lax.rem(me + o, members)}, device_id_type=MESH
        )
        return carry

    lax.fori_loop(1, members, greet, 0)
    blank_ref[...] = jnp.zeros_like(blank_ref)
    spare = pl.ds(recv_ref.shape[0] - 16, 16)
    blank = pltpu.make_async_copy(blank_ref, recv_ref.at[spare], blank_sem)
    blank.start()

    steps = a_ref.shape[0] // step_lanes
    cuts = ((0, 4), (4, steps + 1))

    def gathered(rows):
        return lax.dot_general(
            pick_ref[...], rows, (((1,), (1,)), ((), ())), preferred_element_type=jnp.float32
        ).astype(send_ref.dtype)

    def gather(first, end):
        def body(i, carry):
            at = pl.ds(pl.multiple_of(i * step_lanes, step_lanes), step_lanes)
            send_ref[:, at] = gathered(a_ref[at, :])
            return carry

        lax.fori_loop(first, min(end, steps), body, 0)
        if end > steps:
            send_ref[:, steps * step_lanes :] = gathered(p_ref[...])

    def lanes(n):
        return pl.ds(cuts[n][0] * step_lanes, (cuts[n][1] - cuts[n][0]) * step_lanes)

    def block(i):
        return pl.ds(pl.multiple_of(i * slots, 16), slots)

    def copy(n, o):
        other = lax.rem(me + o, members)
        return pltpu.make_async_remote_copy(
            src_ref=send_ref.at[block(other), lanes(n)],
            dst_ref=recv_ref.at[block(me), lanes(n)],
            send_sem=send_sem.at[n, o],
            recv_sem=recv_sem.at[n, o],
            device_id={"member": other},
            device_id_type=MESH,
        )

    def own(n):
        return pltpu.make_async_copy(
            send_ref.at[block(me), lanes(n)], recv_ref.at[block(me), lanes(n)], own_sem.at[n, 0]
        )

    def start_all(n):
        def start(o, carry):
            copy(n, o).start()
            return carry

        lax.fori_loop(1, members, start, 0)
        own(n).start()

    def finish_all(n):
        def finish(o, carry):
            copy(n, o).wait()
            return carry

        own(n).wait()
        lax.fori_loop(1, members, finish, 0)

    if not spill:
        gather(*cuts[0])
        pl.semaphore_wait(barrier, members - 1)
        start_all(0)
        gather(*cuts[1])
        start_all(1)
        finish_all(0)
        finish_all(1)
        blank.wait()
        return

    chain_send, chain_recv, twin_send, twin_recv = sems
    chips = members // 2
    chip, core = me // 2, me % 2

    def last(n):
        return send_ref.at[pl.ds(members * slots, spill), lanes(n)]

    def shelf(n, origin, side):
        at = members * slots + (origin * 2 + side) * spill
        return recv_ref.at[pl.ds(pl.multiple_of(at, 16), spill), lanes(n)]

    def hop(n, origin, step, src):
        return pltpu.make_async_remote_copy(
            src_ref=src,
            dst_ref=shelf(n, origin, core),
            send_sem=chain_send.at[n, origin, (step + 1) // 2],
            recv_sem=chain_recv.at[n, origin],
            device_id={"member": lax.rem(me + 2 * step + members, members)},
            device_id_type=MESH,
        )

    def twin(n, origin, src, side):
        return pltpu.make_async_remote_copy(
            src_ref=src,
            dst_ref=shelf(n, origin, side),
            send_sem=twin_send.at[n, origin],
            recv_sem=twin_recv.at[n, origin],
            device_id={"member": chip * 2 + 1 - core},
            device_id_type=MESH,
        )

    def own_last(n):
        return pltpu.make_async_copy(last(n), shelf(n, chip, core), own_sem.at[n, 1])

    def has(step):
        return jnp.logical_and(chip + step >= 0, chip + step < chips)

    def launch(n):
        for step in (1, -1):

            @pl.when(has(step))
            def _():
                hop(n, chip, step, last(n)).start()

        twin(n, chip, last(n), core).start()
        own_last(n).start()
        start_all(n)

    gather(*cuts[0])
    pl.semaphore_wait(barrier, members - 1)
    launch(0)
    gather(*cuts[1])
    launch(1)
    for n in range(2):
        for far in range(1, chips):
            for step in (1, -1):
                origin = chip - step * far

                @pl.when(has(-step * far))
                def _():
                    held = shelf(n, origin, core)
                    hop(n, origin, step, held).wait_recv()
                    twin(n, origin, held, core).start()

                    @pl.when(has(step))
                    def _():
                        hop(n, origin, step, held).start()

    for n in range(2):
        own_last(n).wait()
        twin(n, chip, last(n), core).wait_send()
        twin(n, chip, last(n), 1 - core).wait_recv()
        for step in (1, -1):

            @pl.when(has(step))
            def _():
                hop(n, chip, step, last(n)).wait_send()

        for far in range(1, chips):
            for step in (1, -1):
                origin = chip - step * far

                @pl.when(has(-step * far))
                def _():
                    held = shelf(n, origin, core)
                    twin(n, origin, held, core).wait_send()
                    twin(n, origin, held, 1 - core).wait_recv()

                    @pl.when(has(step))
                    def _():
                        hop(n, origin, step, held).wait_send()

        finish_all(n)
    blank.wait()


def exchange(pick, a_rows, p_rows, members, slots, spill, total):
    size, step_lanes = a_rows.shape[0], p_rows.shape[0]
    dma = pltpu.SemaphoreType.DMA
    width = size + step_lanes
    sems = [dma((2, members)), dma((2, members)), dma((2, 2))]
    if spill:
        chips = members // 2
        sems += [dma((2, chips, 2)), dma((2, chips)), dma((2, chips)), dma((2, chips))]
    return pl.pallas_call(
        functools.partial(exchange_kernel, members, slots, spill, step_lanes),
        out_shape=jax.ShapeDtypeStruct((total, width), a_rows.dtype),
        in_specs=[pl.BlockSpec(memory_space=pltpu.VMEM)] * 3,
        out_specs=pl.BlockSpec(memory_space=pl.ANY),
        scratch_shapes=[
            pltpu.VMEM((pick.shape[0], width), a_rows.dtype),
            pltpu.VMEM((16, width), a_rows.dtype),
            dma,
        ]
        + sems,
        compiler_params=pltpu.CompilerParams(
            collective_id=1 if spill else 0,
            has_side_effects=True,
            vmem_limit_bytes=44 * 1024 * 1024,
        ),
        name="exchange_spill" if spill else "exchange_rows",
    )(pick, a_rows, p_rows)


def counts_kernel(groups, members, own_ref, all_ref, send_sem, recv_sem):
    devices = groups * members
    flat = lax.axis_index("group") * members + lax.axis_index("member")
    barrier = pltpu.get_barrier_semaphore()

    def target(o):
        other = lax.rem(flat + o, devices)
        return {"group": other // members, "member": lax.rem(other, members)}

    def greet(o, carry):
        pl.semaphore_signal(barrier, inc=1, device_id=target(o), device_id_type=MESH)
        return carry

    lax.fori_loop(1, devices, greet, 0)
    pl.semaphore_wait(barrier, devices - 1)

    def copy(o):
        return pltpu.make_async_remote_copy(
            src_ref=own_ref,
            dst_ref=all_ref.at[flat],
            send_sem=send_sem.at[o],
            recv_sem=recv_sem.at[o],
            device_id=target(o),
            device_id_type=MESH,
        )

    def start(o, carry):
        copy(o).start()
        return carry

    def finish(o, carry):
        copy(o).wait()
        return carry

    lax.fori_loop(1, devices, start, 0)
    all_ref[flat] = own_ref[...]
    lax.fori_loop(1, devices, finish, 0)


def share_counts(counts, groups, members):
    devices = groups * members
    own = jnp.pad(counts, (0, LANES - members))[None, :]
    return pl.pallas_call(
        functools.partial(counts_kernel, groups, members),
        out_shape=jax.ShapeDtypeStruct((devices, 1, LANES), counts.dtype),
        in_specs=[pl.BlockSpec(memory_space=pltpu.VMEM)],
        out_specs=pl.BlockSpec(memory_space=pltpu.VMEM),
        scratch_shapes=[pltpu.SemaphoreType.DMA((devices,))] * 2,
        compiler_params=pltpu.CompilerParams(collective_id=2, has_side_effects=True),
        name="share_counts",
    )(own)[:, 0, :members]


def shifted(x, k):
    width = x.shape[-1]
    if k == 0:
        return pltpu.roll(x, 1, axis=x.ndim - 1)
    if k == 2:
        return pltpu.roll(x, width - 1, axis=x.ndim - 1)
    return x


def setup_kernel(ext_ref, s_ref, co_ref, p3, s3, ap3, dinv, tiles, wide):
    _, modes, tile, rows = s_ref.shape
    width = ext_ref.shape[1]
    f32 = jnp.float32
    half = tile // 2
    parts = [(i, l) for l in range(width // LANES) for i in range(2)]
    line = lax.broadcasted_iota(jnp.int32, (tile, width), 0)

    def pick_diag(j, total):
        at = pl.multiple_of((tile + j) * tile, tile)
        return total + jnp.where(line == j, ext_ref[pl.ds(at, tile), :].astype(f32), 0.0)

    diag = lax.fori_loop(0, tile, pick_diag, jnp.zeros((tile, width), f32))
    dinv[...] = jnp.where(diag > 1.0, 1.0 / jnp.where(diag > 1.0, diag, 1.0), 0.0)
    for c in range(modes):
        own = ext_ref[pl.ds((3 * tile + c) * tile, tile), :].astype(f32)
        for k in range(3):
            p3[k, c] = shifted(own, k)

    def product(ks, rows, i0, l0):
        lanes = pl.ds(l0, LANES)

        def body(j8, accs):
            accs = list(accs)
            j0 = pl.multiple_of(j8 * 8, 8)
            for k in ks:
                vecs = [ref[pl.ds(j0, 8), lanes] for ref in rows(k)]
                for jj in range(8):
                    at = pl.multiple_of((k * tile + j0 + jj) * tile + i0, half)
                    a = ext_ref[pl.ds(at, half), lanes].astype(f32)
                    for c in range(modes):
                        accs[c] = accs[c] + a * vecs[c][jj : jj + 1]
            return tuple(accs)

        zero = jnp.zeros((half, LANES), f32)
        return lax.fori_loop(0, tile // 8, body, (zero,) * modes)

    def each_part(fn):
        def body(q, carry):
            fn(
                pl.multiple_of((q % 2) * half, half),
                pl.multiple_of((q // 2) * LANES, LANES),
            )
            return carry

        lax.fori_loop(0, len(parts), body, 0)

    for k in range(3):

        def smooth(i0, l0, k=k):
            accs = product([k], lambda k: [p3.at[k, c] for c in range(modes)], i0, l0)
            inv = 0.6 * dinv[pl.ds(i0, half), pl.ds(l0, LANES)]
            for c in range(modes):
                value = -inv * accs[c]
                if k == 1:
                    value = p3[1, c, pl.ds(i0, half), pl.ds(l0, LANES)] + value
                value = value.astype(jnp.bfloat16)
                s3[1, k, c, pl.ds(i0, half), pl.ds(l0, LANES)] = value.astype(f32)

        each_part(smooth)

    def spread_s(q, carry):
        t, c = q // modes, q % modes
        own = s3[1, t, c]
        s_ref[t, c] = pltpu.roll(own, width - HALO, axis=1)[:, :rows].astype(jnp.bfloat16)
        s3[0, t, c] = shifted(own, 0)
        s3[2, t, c] = shifted(own, 2)
        return carry

    lax.fori_loop(0, 3 * modes, spread_s, 0)

    for e in range(5):

        def prod(i0, l0, e=e):
            ks = [k for k in range(3) if 0 <= e - k <= 2]
            accs = product(ks, lambda k: [s3.at[k, e - k, c] for c in range(modes)], i0, l0)
            for c in range(modes):
                ap3[1, e, c, pl.ds(i0, half), pl.ds(l0, LANES)] = (
                    accs[c].astype(jnp.bfloat16).astype(f32)
                )

        each_part(prod)

    def spread_ap(q, carry):
        e, c = q // modes, q % modes
        own = ap3[1, e, c]
        ap3[0, e, c] = shifted(own, 0)
        ap3[2, e, c] = shifted(own, 2)
        return carry

    lax.fori_loop(0, 5 * modes, spread_ap, 0)

    for f in range(7):

        def coarse(q, carry, f=f):
            c, l0 = q // (width // LANES), pl.multiple_of((q % (width // LANES)) * LANES, LANES)
            lanes = pl.ds(l0, LANES)
            sums = [None] * modes
            for dn in (-1, 0, 1):
                e = f - 1 - dn
                if not 0 <= e <= 4:
                    continue
                s = s3[dn + 1, 1 - dn, c, :, lanes]
                for d in range(modes):
                    term = s * ap3[dn + 1, e, d, :, lanes]
                    term = jnp.sum(term.reshape(tile // 8, 8, LANES), axis=0)
                    sums[d] = term if sums[d] is None else sums[d] + term
            for d in range(modes):
                tiles[f, c, d : d + 1, lanes] = jnp.sum(sums[d], axis=0, keepdims=True)
            return carry

        lax.fori_loop(0, modes * (width // LANES), coarse, 0)

    count = 7 * modes * modes
    for f in range(7):
        for c in range(modes):
            at = (f * modes + c) * modes
            wide[at : at + modes, :] = tiles[f, c]
    wide[count:] = jnp.zeros((wide.shape[0] - count, width), f32)
    co_ref[...] = jnp.transpose(pltpu.roll(wide[...], width - HALO, axis=1))[:rows, :count]


def setup(ext, modes, tile, rows):
    width = ext.shape[1]
    count = 7 * modes * modes
    f32 = jnp.float32
    return pl.pallas_call(
        setup_kernel,
        out_shape=(
            jax.ShapeDtypeStruct((3, modes, tile, rows), jnp.bfloat16),
            jax.ShapeDtypeStruct((rows, count), f32),
        ),
        in_specs=[pl.BlockSpec(memory_space=pltpu.VMEM)],
        out_specs=(pl.BlockSpec(memory_space=pltpu.VMEM),) * 2,
        scratch_shapes=[
            pltpu.VMEM((3, modes, tile, width), f32),
            pltpu.VMEM((3, 3, modes, tile, width), f32),
            pltpu.VMEM((3, 5, modes, tile, width), f32),
            pltpu.VMEM((tile, width), f32),
            pltpu.VMEM((7, modes, modes, width), f32),
            pltpu.VMEM((-(-count // LANES) * LANES, width), f32),
        ],
        compiler_params=pltpu.CompilerParams(vmem_limit_bytes=28 * 1024 * 1024),
        name="coarse_setup",
    )(ext)


def per_device(a_band, p_tent, new_owner):
    members = lax.axis_size("member")
    groups = lax.axis_size("group")
    me = lax.axis_index("member")
    rows, _, tile, _ = a_band.shape
    modes = p_tent.shape[1]
    cap = 2 * rows // members
    slots = -(-cap // 16) * 16
    bf16, i32 = jnp.bfloat16, jnp.int32
    size = 3 * tile * tile
    width = -(-(rows + 2 * HALO) // LANES) * LANES
    spill = 16 if slots > 32 and members % 2 == 0 else 0
    few = slots - spill
    total = max(members * slots, members * (few + spill))

    onehot = (new_owner[None, :] == jnp.arange(members, dtype=i32)[:, None]).astype(i32)
    earlier = (jnp.arange(rows)[:, None] < jnp.arange(rows)[None, :]).astype(jnp.float32)
    before = jnp.dot(onehot.astype(jnp.float32), earlier).astype(i32)
    place = jnp.sum(before * onehot, 0)
    counts = jnp.sum(onehot, 1)
    axes = ("group", "member")
    if spill:
        every = share_counts(counts, groups, members)
        table = lax.dynamic_slice_in_dim(every, lax.axis_index("group") * members, members, 0)
    else:
        table = lax.all_gather(counts, "member")
    got = lax.dynamic_index_in_dim(table, me, 1, keepdims=False)

    a_rows = a_band.transpose(1, 3, 2, 0).reshape(size, rows)
    p_rows = p_tent.transpose(1, 2, 0).reshape(modes * tile, rows)
    member = jnp.arange(members)
    upto = member[None, :] <= member[:, None]
    starts = jnp.sum(jnp.where(upto, got[None, :], 0), 1) - got

    def picked(flat_slot, count):
        return (jnp.arange(count, dtype=i32)[:, None] == flat_slot[None, :]).astype(bf16)

    flat_slot = new_owner * slots + place

    def direct(own_a, own_p):
        pick = picked(flat_slot, members * slots)
        return exchange(pick, own_a, own_p, members, slots, 0, total + 16)

    def direct_lands():
        within = jnp.arange(slots, dtype=i32)
        lands = jnp.where(within[None, :] < got[:, None], starts[:, None] + within[None, :], -width)
        return jnp.pad(lands.reshape(-1), (0, total - members * slots), constant_values=-width)

    if spill:
        over = jnp.maximum(every - few, 0)
        fits = jnp.max(jnp.sum(over, 1)) <= spill

        mine = jnp.maximum(counts - few, 0)
        first = jnp.sum(jnp.where(upto, mine[None, :], 0), 1) - mine
        base = jnp.sum(first[:, None] * onehot, 0)
        spill_slot = jnp.where(
            place < few, new_owner * few + place, members * few + base + place - few
        )

        def spilled(own_a, own_p):
            pick = picked(spill_slot, members * few + spill)
            return exchange(pick, own_a, own_p, members, few, spill, total + 16)

        def spilled_lands():
            within = jnp.arange(few, dtype=i32)
            head = jnp.where(
                within[None, :] < got[:, None], starts[:, None] + within[None, :], -width
            )
            over_group = jnp.maximum(table - few, 0)
            before_me = jnp.sum(jnp.where(member[None, :] < me, over_group, 0), 1)
            at = jnp.arange(spill, dtype=i32)[None, :] - before_me[:, None]
            good = jnp.logical_and(at >= 0, at < jnp.maximum(got - few, 0)[:, None])
            tail = jnp.where(good, starts[:, None] + few + at, -width)
            lands = jnp.concatenate([head.reshape(-1), tail.reshape(-1)])
            return jnp.pad(lands, (0, total - members * (few + spill)), constant_values=-width)

        lands = jnp.where(fits, spilled_lands(), direct_lands())
        recv = lax.cond(fits, spilled, direct, a_rows, p_rows)
    else:
        lands = direct_lands()
        recv = direct(a_rows, p_rows)

    edge = jnp.arange(16, dtype=i32)
    edge_row = jnp.where(edge < HALO, edge, jnp.where(edge < 2 * HALO, rows - 2 * HALO + edge, -1))
    filled = jnp.concatenate([lands, jnp.full((16,), -width, i32)])
    rim_pick = (edge_row[:, None] == filled[None, :]).astype(bf16)
    rim = jnp.dot(rim_pick, recv, preferred_element_type=jnp.float32).astype(bf16)
    devices = groups * members
    up = [(i, i + 1) for i in range(devices - 1)]
    down = [(i + 1, i) for i in range(devices - 1)]
    from_left = lax.ppermute(rim[HALO : 2 * HALO], axes, up)
    from_right = lax.ppermute(rim[:HALO], axes, down)
    halo = jnp.concatenate(
        [from_left, from_right, jnp.zeros((16 - 2 * HALO, rim.shape[1]), bf16)], 0
    )
    recv = lax.dynamic_update_slice(recv, halo, (total, 0))
    halo_lane = jnp.where(edge < HALO, edge, jnp.where(edge < 2 * HALO, rows + edge, -1))
    lane = jnp.concatenate([lands + HALO, halo_lane])
    place_out = (lane[:, None] == jnp.arange(width, dtype=i32)[None, :]).astype(bf16)
    ext = lax.dot_general(
        recv, place_out, (((0,), (0,)), ((), ())), preferred_element_type=jnp.float32
    ).astype(bf16)
    s_out, coarse = setup(ext, modes, tile, rows)
    return (s_out.transpose(3, 0, 1, 2), coarse)


def solution(mesh):
    in_specs = (
        P(("group", "member"), None, None, None),
        P(("group", "member"), None, None),
        P(("group", "member")),
    )
    out_specs = (P(("group", "member"), None, None, None), P(("group", "member"), None))
    return jax.shard_map(
        per_device, mesh=mesh, in_specs=in_specs, out_specs=out_specs, check_vma=False
    )
```

```python
import functools

import jax
import jax.numpy as jnp
from jax import lax
from jax.experimental import pallas as pl
from jax.experimental.pallas import tpu as pltpu
from jax.sharding import PartitionSpec as P

HALO = 3
LANES = 128
MESH = pl.DeviceIdType.MESH


def exchange_kernel(
    members, slots, spill, step_lanes, pick_ref, a_ref, p_ref, recv_ref, send_ref, blank_ref,
    blank_sem, send_sem, recv_sem, own_sem, *sems
):
    me = lax.axis_index("member")
    barrier = pltpu.get_barrier_semaphore()

    def greet(o, carry):
        pl.semaphore_signal(
            barrier, inc=1, device_id={"member": lax.rem(me + o, members)}, device_id_type=MESH
        )
        return carry

    lax.fori_loop(1, members, greet, 0)
    blank_ref[...] = jnp.zeros_like(blank_ref)
    spare = pl.ds(recv_ref.shape[0] - 16, 16)
    blank = pltpu.make_async_copy(blank_ref, recv_ref.at[spare], blank_sem)
    blank.start()

    steps = a_ref.shape[0] // step_lanes
    cuts = ((0, 4), (4, steps + 1))

    def gathered(rows):
        return lax.dot_general(
            pick_ref[...], rows, (((1,), (1,)), ((), ())), preferred_element_type=jnp.float32
        ).astype(send_ref.dtype)

    def gather(first, end):
        def body(i, carry):
            at = pl.ds(pl.multiple_of(i * step_lanes, step_lanes), step_lanes)
            send_ref[:, at] = gathered(a_ref[at, :])
            return carry

        lax.fori_loop(first, min(end, steps), body, 0)
        if end > steps:
            send_ref[:, steps * step_lanes :] = gathered(p_ref[...])

    def lanes(n):
        return pl.ds(cuts[n][0] * step_lanes, (cuts[n][1] - cuts[n][0]) * step_lanes)

    def block(i):
        return pl.ds(pl.multiple_of(i * slots, 16), slots)

    def copy(n, o):
        other = lax.rem(me + o, members)
        return pltpu.make_async_remote_copy(
            src_ref=send_ref.at[block(other), lanes(n)],
            dst_ref=recv_ref.at[block(me), lanes(n)],
            send_sem=send_sem.at[n, o],
            recv_sem=recv_sem.at[n, o],
            device_id={"member": other},
            device_id_type=MESH,
        )

    def own(n):
        return pltpu.make_async_copy(
            send_ref.at[block(me), lanes(n)], recv_ref.at[block(me), lanes(n)], own_sem.at[n, 0]
        )

    def start_all(n):
        def start(i, carry):
            far = members // 2 + jnp.where(i % 2 == 1, (i + 1) // 2, -(i // 2))
            copy(n, far).start()
            return carry

        lax.fori_loop(0, members - 1, start, 0)
        own(n).start()

    def finish_all(n):
        def finish(o, carry):
            copy(n, o).wait()
            return carry

        own(n).wait()
        lax.fori_loop(1, members, finish, 0)

    if not spill:
        gather(*cuts[0])
        pl.semaphore_wait(barrier, members - 1)
        start_all(0)
        gather(*cuts[1])
        start_all(1)
        finish_all(0)
        finish_all(1)
        blank.wait()
        return

    chain_send, chain_recv, twin_send, twin_recv = sems
    chips = members // 2
    chip, core = me // 2, me % 2

    def last(n):
        return send_ref.at[pl.ds(members * slots, spill), lanes(n)]

    def shelf(n, origin, side):
        at = members * slots + (origin * 2 + side) * spill
        return recv_ref.at[pl.ds(pl.multiple_of(at, 16), spill), lanes(n)]

    def hop(n, origin, step, src):
        return pltpu.make_async_remote_copy(
            src_ref=src,
            dst_ref=shelf(n, origin, core),
            send_sem=chain_send.at[n, origin, (step + 1) // 2],
            recv_sem=chain_recv.at[n, origin],
            device_id={"member": lax.rem(me + 2 * step + members, members)},
            device_id_type=MESH,
        )

    def twin(n, origin, src, side):
        return pltpu.make_async_remote_copy(
            src_ref=src,
            dst_ref=shelf(n, origin, side),
            send_sem=twin_send.at[n, origin],
            recv_sem=twin_recv.at[n, origin],
            device_id={"member": chip * 2 + 1 - core},
            device_id_type=MESH,
        )

    def own_last(n):
        return pltpu.make_async_copy(last(n), shelf(n, chip, core), own_sem.at[n, 1])

    def has(step):
        return jnp.logical_and(chip + step >= 0, chip + step < chips)

    def launch(n):
        for step in (1, -1):

            @pl.when(has(step))
            def _():
                hop(n, chip, step, last(n)).start()

        twin(n, chip, last(n), core).start()
        own_last(n).start()
        start_all(n)

    gather(*cuts[0])
    pl.semaphore_wait(barrier, members - 1)
    launch(0)
    gather(*cuts[1])
    launch(1)
    for n in range(2):
        for far in range(1, chips):
            for step in (1, -1):
                origin = chip - step * far

                @pl.when(has(-step * far))
                def _():
                    held = shelf(n, origin, core)
                    hop(n, origin, step, held).wait_recv()
                    twin(n, origin, held, core).start()

                    @pl.when(has(step))
                    def _():
                        hop(n, origin, step, held).start()

    for n in range(2):
        own_last(n).wait()
        twin(n, chip, last(n), core).wait_send()
        twin(n, chip, last(n), 1 - core).wait_recv()
        for step in (1, -1):

            @pl.when(has(step))
            def _():
                hop(n, chip, step, last(n)).wait_send()

        for far in range(1, chips):
            for step in (1, -1):
                origin = chip - step * far

                @pl.when(has(-step * far))
                def _():
                    held = shelf(n, origin, core)
                    twin(n, origin, held, core).wait_send()
                    twin(n, origin, held, 1 - core).wait_recv()

                    @pl.when(has(step))
                    def _():
                        hop(n, origin, step, held).wait_send()

        finish_all(n)
    blank.wait()


def exchange(pick, a_rows, p_rows, members, slots, spill, total):
    size, step_lanes = a_rows.shape[0], p_rows.shape[0]
    dma = pltpu.SemaphoreType.DMA
    width = size + step_lanes
    sems = [dma((2, members)), dma((2, members)), dma((2, 2))]
    if spill:
        chips = members // 2
        sems += [dma((2, chips, 2)), dma((2, chips)), dma((2, chips)), dma((2, chips))]
    return pl.pallas_call(
        functools.partial(exchange_kernel, members, slots, spill, step_lanes),
        out_shape=jax.ShapeDtypeStruct((total, width), a_rows.dtype),
        in_specs=[pl.BlockSpec(memory_space=pltpu.VMEM)] * 3,
        out_specs=pl.BlockSpec(memory_space=pl.ANY),
        scratch_shapes=[
            pltpu.VMEM((pick.shape[0], width), a_rows.dtype),
            pltpu.VMEM((16, width), a_rows.dtype),
            dma,
        ]
        + sems,
        compiler_params=pltpu.CompilerParams(
            collective_id=1 if spill else 0,
            has_side_effects=True,
            vmem_limit_bytes=44 * 1024 * 1024,
        ),
        name="exchange_spill" if spill else "exchange_rows",
    )(pick, a_rows, p_rows)


def counts_kernel(groups, members, own_ref, all_ref, send_sem, recv_sem):
    devices = groups * members
    flat = lax.axis_index("group") * members + lax.axis_index("member")
    barrier = pltpu.get_barrier_semaphore()

    def target(o):
        other = lax.rem(flat + o, devices)
        return {"group": other // members, "member": lax.rem(other, members)}

    def greet(o, carry):
        pl.semaphore_signal(barrier, inc=1, device_id=target(o), device_id_type=MESH)
        return carry

    lax.fori_loop(1, devices, greet, 0)
    pl.semaphore_wait(barrier, devices - 1)

    def copy(o):
        return pltpu.make_async_remote_copy(
            src_ref=own_ref,
            dst_ref=all_ref.at[flat],
            send_sem=send_sem.at[o],
            recv_sem=recv_sem.at[o],
            device_id=target(o),
            device_id_type=MESH,
        )

    def start(o, carry):
        copy(o).start()
        return carry

    def finish(o, carry):
        copy(o).wait()
        return carry

    lax.fori_loop(1, devices, start, 0)
    all_ref[flat] = own_ref[...]
    lax.fori_loop(1, devices, finish, 0)


def share_counts(counts, groups, members):
    devices = groups * members
    own = jnp.pad(counts, (0, LANES - members))[None, :]
    return pl.pallas_call(
        functools.partial(counts_kernel, groups, members),
        out_shape=jax.ShapeDtypeStruct((devices, 1, LANES), counts.dtype),
        in_specs=[pl.BlockSpec(memory_space=pltpu.VMEM)],
        out_specs=pl.BlockSpec(memory_space=pltpu.VMEM),
        scratch_shapes=[pltpu.SemaphoreType.DMA((devices,))] * 2,
        compiler_params=pltpu.CompilerParams(collective_id=2, has_side_effects=True),
        name="share_counts",
    )(own)[:, 0, :members]


def shifted(x, k):
    width = x.shape[-1]
    if k == 0:
        return pltpu.roll(x, 1, axis=x.ndim - 1)
    if k == 2:
        return pltpu.roll(x, width - 1, axis=x.ndim - 1)
    return x


def setup_kernel(ext_ref, s_ref, co_ref, p3, s3, ap3, dinv, tiles, wide):
    _, modes, tile, rows = s_ref.shape
    width = ext_ref.shape[1]
    f32 = jnp.float32
    half = tile // 2
    parts = [(i, l) for l in range(width // LANES) for i in range(2)]
    line = lax.broadcasted_iota(jnp.int32, (tile, width), 0)

    def pick_diag(j, total):
        at = pl.multiple_of((tile + j) * tile, tile)
        return total + jnp.where(line == j, ext_ref[pl.ds(at, tile), :].astype(f32), 0.0)

    diag = lax.fori_loop(0, tile, pick_diag, jnp.zeros((tile, width), f32))
    dinv[...] = jnp.where(diag > 1.0, 1.0 / jnp.where(diag > 1.0, diag, 1.0), 0.0)
    for c in range(modes):
        own = ext_ref[pl.ds((3 * tile + c) * tile, tile), :].astype(f32)
        for k in range(3):
            p3[k, c] = shifted(own, k)

    def product(ks, rows, i0, l0):
        lanes = pl.ds(l0, LANES)

        def body(j8, accs):
            accs = list(accs)
            j0 = pl.multiple_of(j8 * 8, 8)
            for k in ks:
                vecs = [ref[pl.ds(j0, 8), lanes] for ref in rows(k)]
                for jj in range(8):
                    at = pl.multiple_of((k * tile + j0 + jj) * tile + i0, half)
                    a = ext_ref[pl.ds(at, half), lanes].astype(f32)
                    for c in range(modes):
                        accs[c] = accs[c] + a * vecs[c][jj : jj + 1]
            return tuple(accs)

        zero = jnp.zeros((half, LANES), f32)
        return lax.fori_loop(0, tile // 8, body, (zero,) * modes)

    def each_part(fn):
        def body(q, carry):
            fn(
                pl.multiple_of((q % 2) * half, half),
                pl.multiple_of((q // 2) * LANES, LANES),
            )
            return carry

        lax.fori_loop(0, len(parts), body, 0)

    for k in range(3):

        def smooth(i0, l0, k=k):
            accs = product([k], lambda k: [p3.at[k, c] for c in range(modes)], i0, l0)
            inv = 0.6 * dinv[pl.ds(i0, half), pl.ds(l0, LANES)]
            for c in range(modes):
                value = -inv * accs[c]
                if k == 1:
                    value = p3[1, c, pl.ds(i0, half), pl.ds(l0, LANES)] + value
                value = value.astype(jnp.bfloat16)
                s3[1, k, c, pl.ds(i0, half), pl.ds(l0, LANES)] = value.astype(f32)

        each_part(smooth)

    def spread_s(q, carry):
        t, c = q // modes, q % modes
        own = s3[1, t, c]
        s_ref[t, c] = pltpu.roll(own, width - HALO, axis=1)[:, :rows].astype(jnp.bfloat16)
        s3[0, t, c] = shifted(own, 0)
        s3[2, t, c] = shifted(own, 2)
        return carry

    lax.fori_loop(0, 3 * modes, spread_s, 0)

    for e in range(5):

        def prod(i0, l0, e=e):
            ks = [k for k in range(3) if 0 <= e - k <= 2]
            accs = product(ks, lambda k: [s3.at[k, e - k, c] for c in range(modes)], i0, l0)
            for c in range(modes):
                ap3[1, e, c, pl.ds(i0, half), pl.ds(l0, LANES)] = (
                    accs[c].astype(jnp.bfloat16).astype(f32)
                )

        each_part(prod)

    def spread_ap(q, carry):
        e, c = q // modes, q % modes
        own = ap3[1, e, c]
        ap3[0, e, c] = shifted(own, 0)
        ap3[2, e, c] = shifted(own, 2)
        return carry

    lax.fori_loop(0, 5 * modes, spread_ap, 0)

    for f in range(7):

        def coarse(q, carry, f=f):
            c, l0 = q // (width // LANES), pl.multiple_of((q % (width // LANES)) * LANES, LANES)
            lanes = pl.ds(l0, LANES)
            sums = [None] * modes
            for dn in (-1, 0, 1):
                e = f - 1 - dn
                if not 0 <= e <= 4:
                    continue
                s = s3[dn + 1, 1 - dn, c, :, lanes]
                for d in range(modes):
                    term = s * ap3[dn + 1, e, d, :, lanes]
                    term = jnp.sum(term.reshape(tile // 8, 8, LANES), axis=0)
                    sums[d] = term if sums[d] is None else sums[d] + term
            for d in range(modes):
                tiles[f, c, d : d + 1, lanes] = jnp.sum(sums[d], axis=0, keepdims=True)
            return carry

        lax.fori_loop(0, modes * (width // LANES), coarse, 0)

    count = 7 * modes * modes
    for f in range(7):
        for c in range(modes):
            at = (f * modes + c) * modes
            wide[at : at + modes, :] = tiles[f, c]
    wide[count:] = jnp.zeros((wide.shape[0] - count, width), f32)
    co_ref[...] = jnp.transpose(pltpu.roll(wide[...], width - HALO, axis=1))[:rows, :count]


def setup(ext, modes, tile, rows):
    width = ext.shape[1]
    count = 7 * modes * modes
    f32 = jnp.float32
    return pl.pallas_call(
        setup_kernel,
        out_shape=(
            jax.ShapeDtypeStruct((3, modes, tile, rows), jnp.bfloat16),
            jax.ShapeDtypeStruct((rows, count), f32),
        ),
        in_specs=[pl.BlockSpec(memory_space=pltpu.VMEM)],
        out_specs=(pl.BlockSpec(memory_space=pltpu.VMEM),) * 2,
        scratch_shapes=[
            pltpu.VMEM((3, modes, tile, width), f32),
            pltpu.VMEM((3, 3, modes, tile, width), f32),
            pltpu.VMEM((3, 5, modes, tile, width), f32),
            pltpu.VMEM((tile, width), f32),
            pltpu.VMEM((7, modes, modes, width), f32),
            pltpu.VMEM((-(-count // LANES) * LANES, width), f32),
        ],
        compiler_params=pltpu.CompilerParams(vmem_limit_bytes=28 * 1024 * 1024),
        name="coarse_setup",
    )(ext)


def per_device(a_band, p_tent, new_owner):
    members = lax.axis_size("member")
    groups = lax.axis_size("group")
    me = lax.axis_index("member")
    rows, _, tile, _ = a_band.shape
    modes = p_tent.shape[1]
    cap = 2 * rows // members
    slots = -(-cap // 16) * 16
    bf16, i32 = jnp.bfloat16, jnp.int32
    size = 3 * tile * tile
    width = -(-(rows + 2 * HALO) // LANES) * LANES
    spill = 16 if slots > 32 and members % 2 == 0 else 0
    few = slots - spill
    total = max(members * slots, members * (few + spill))

    onehot = (new_owner[None, :] == jnp.arange(members, dtype=i32)[:, None]).astype(i32)
    earlier = (jnp.arange(rows)[:, None] < jnp.arange(rows)[None, :]).astype(jnp.float32)
    before = jnp.dot(onehot.astype(jnp.float32), earlier).astype(i32)
    place = jnp.sum(before * onehot, 0)
    counts = jnp.sum(onehot, 1)
    axes = ("group", "member")
    if spill:
        every = share_counts(counts, groups, members)
        table = lax.dynamic_slice_in_dim(every, lax.axis_index("group") * members, members, 0)
    else:
        table = lax.all_gather(counts, "member")
    got = lax.dynamic_index_in_dim(table, me, 1, keepdims=False)

    a_rows = a_band.transpose(1, 3, 2, 0).reshape(size, rows)
    p_rows = p_tent.transpose(1, 2, 0).reshape(modes * tile, rows)
    member = jnp.arange(members)
    upto = member[None, :] <= member[:, None]
    starts = jnp.sum(jnp.where(upto, got[None, :], 0), 1) - got

    def picked(flat_slot, count):
        return (jnp.arange(count, dtype=i32)[:, None] == flat_slot[None, :]).astype(bf16)

    flat_slot = new_owner * slots + place

    def direct(own_a, own_p):
        pick = picked(flat_slot, members * slots)
        return exchange(pick, own_a, own_p, members, slots, 0, total + 16)

    def direct_lands():
        within = jnp.arange(slots, dtype=i32)
        lands = jnp.where(within[None, :] < got[:, None], starts[:, None] + within[None, :], -width)
        return jnp.pad(lands.reshape(-1), (0, total - members * slots), constant_values=-width)

    if spill:
        over = jnp.maximum(every - few, 0)
        fits = jnp.max(jnp.sum(over, 1)) <= spill

        mine = jnp.maximum(counts - few, 0)
        first = jnp.sum(jnp.where(upto, mine[None, :], 0), 1) - mine
        base = jnp.sum(first[:, None] * onehot, 0)
        spill_slot = jnp.where(
            place < few, new_owner * few + place, members * few + base + place - few
        )

        def spilled(own_a, own_p):
            pick = picked(spill_slot, members * few + spill)
            return exchange(pick, own_a, own_p, members, few, spill, total + 16)

        def spilled_lands():
            within = jnp.arange(few, dtype=i32)
            head = jnp.where(
                within[None, :] < got[:, None], starts[:, None] + within[None, :], -width
            )
            over_group = jnp.maximum(table - few, 0)
            before_me = jnp.sum(jnp.where(member[None, :] < me, over_group, 0), 1)
            at = jnp.arange(spill, dtype=i32)[None, :] - before_me[:, None]
            good = jnp.logical_and(at >= 0, at < jnp.maximum(got - few, 0)[:, None])
            tail = jnp.where(good, starts[:, None] + few + at, -width)
            lands = jnp.concatenate([head.reshape(-1), tail.reshape(-1)])
            return jnp.pad(lands, (0, total - members * (few + spill)), constant_values=-width)

        lands = jnp.where(fits, spilled_lands(), direct_lands())
        recv = lax.cond(fits, spilled, direct, a_rows, p_rows)
    else:
        lands = direct_lands()
        recv = direct(a_rows, p_rows)

    edge = jnp.arange(16, dtype=i32)
    edge_row = jnp.where(edge < HALO, edge, jnp.where(edge < 2 * HALO, rows - 2 * HALO + edge, -1))
    filled = jnp.concatenate([lands, jnp.full((16,), -width, i32)])
    rim_pick = (edge_row[:, None] == filled[None, :]).astype(bf16)
    rim = jnp.dot(rim_pick, recv, preferred_element_type=jnp.float32).astype(bf16)
    devices = groups * members
    up = [(i, i + 1) for i in range(devices - 1)]
    down = [(i + 1, i) for i in range(devices - 1)]
    from_left = lax.ppermute(rim[HALO : 2 * HALO], axes, up)
    from_right = lax.ppermute(rim[:HALO], axes, down)
    halo = jnp.concatenate(
        [from_left, from_right, jnp.zeros((16 - 2 * HALO, rim.shape[1]), bf16)], 0
    )
    recv = lax.dynamic_update_slice(recv, halo, (total, 0))
    halo_lane = jnp.where(edge < HALO, edge, jnp.where(edge < 2 * HALO, rows + edge, -1))
    lane = jnp.concatenate([lands + HALO, halo_lane])
    place_out = (lane[:, None] == jnp.arange(width, dtype=i32)[None, :]).astype(bf16)
    ext = lax.dot_general(
        recv, place_out, (((0,), (0,)), ((), ())), preferred_element_type=jnp.float32
    ).astype(bf16)
    s_out, coarse = setup(ext, modes, tile, rows)
    return (s_out.transpose(3, 0, 1, 2), coarse)


def solution(mesh):
    in_specs = (
        P(("group", "member"), None, None, None),
        P(("group", "member"), None, None),
        P(("group", "member")),
    )
    out_specs = (P(("group", "member"), None, None, None), P(("group", "member"), None))
    return jax.shard_map(
        per_device, mesh=mesh, in_specs=in_specs, out_specs=out_specs, check_vma=False
    )
```

```python
import functools

import jax
import jax.numpy as jnp
from jax import lax
from jax.experimental import pallas as pl
from jax.experimental.pallas import tpu as pltpu
from jax.sharding import PartitionSpec as P

HALO = 3
LANES = 128
MESH = pl.DeviceIdType.MESH


def exchange_kernel(
    members, slots, spill, step_lanes, pick_ref, a_ref, p_ref, recv_ref, send_ref, blank_ref,
    blank_sem, send_sem, recv_sem, own_sem, *sems
):
    me = lax.axis_index("member")
    barrier = pltpu.get_barrier_semaphore()

    def greet(o, carry):
        pl.semaphore_signal(
            barrier, inc=1, device_id={"member": lax.rem(me + o, members)}, device_id_type=MESH
        )
        return carry

    lax.fori_loop(1, members, greet, 0)
    blank_ref[...] = jnp.zeros_like(blank_ref)
    spare = pl.ds(recv_ref.shape[0] - 16, 16)
    blank = pltpu.make_async_copy(blank_ref, recv_ref.at[spare], blank_sem)
    blank.start()

    steps = a_ref.shape[0] // step_lanes
    cuts = ((0, 2), (2, steps + 1))

    def gathered(rows):
        return lax.dot_general(
            pick_ref[...], rows, (((1,), (1,)), ((), ())), preferred_element_type=jnp.float32
        ).astype(send_ref.dtype)

    def gather(first, end):
        def body(i, carry):
            at = pl.ds(pl.multiple_of(i * step_lanes, step_lanes), step_lanes)
            send_ref[:, at] = gathered(a_ref[at, :])
            return carry

        lax.fori_loop(first, min(end, steps), body, 0)
        if end > steps:
            send_ref[:, steps * step_lanes :] = gathered(p_ref[...])

    def lanes(n):
        return pl.ds(cuts[n][0] * step_lanes, (cuts[n][1] - cuts[n][0]) * step_lanes)

    def block(i):
        return pl.ds(pl.multiple_of(i * slots, 16), slots)

    def copy(n, o):
        other = lax.rem(me + o, members)
        return pltpu.make_async_remote_copy(
            src_ref=send_ref.at[block(other), lanes(n)],
            dst_ref=recv_ref.at[block(me), lanes(n)],
            send_sem=send_sem.at[n, o],
            recv_sem=recv_sem.at[n, o],
            device_id={"member": other},
            device_id_type=MESH,
        )

    def own(n):
        return pltpu.make_async_copy(
            send_ref.at[block(me), lanes(n)], recv_ref.at[block(me), lanes(n)], own_sem.at[n, 0]
        )

    def start_all(n):
        def start(i, carry):
            far = members // 2 + jnp.where(i % 2 == 1, (i + 1) // 2, -(i // 2))
            copy(n, far).start()
            return carry

        lax.fori_loop(0, members - 1, start, 0)
        own(n).start()

    def finish_all(n):
        def finish(o, carry):
            copy(n, o).wait()
            return carry

        own(n).wait()
        lax.fori_loop(1, members, finish, 0)

    if not spill:
        gather(*cuts[0])
        pl.semaphore_wait(barrier, members - 1)
        start_all(0)
        gather(*cuts[1])
        start_all(1)
        finish_all(0)
        finish_all(1)
        blank.wait()
        return

    chain_send, chain_recv, twin_send, twin_recv = sems
    chips = members // 2
    chip, core = me // 2, me % 2

    def last(n):
        return send_ref.at[pl.ds(members * slots, spill), lanes(n)]

    def shelf(n, origin, side):
        at = members * slots + (origin * 2 + side) * spill
        return recv_ref.at[pl.ds(pl.multiple_of(at, 16), spill), lanes(n)]

    def hop(n, origin, step, src):
        return pltpu.make_async_remote_copy(
            src_ref=src,
            dst_ref=shelf(n, origin, core),
            send_sem=chain_send.at[n, origin, (step + 1) // 2],
            recv_sem=chain_recv.at[n, origin],
            device_id={"member": lax.rem(me + 2 * step + members, members)},
            device_id_type=MESH,
        )

    def twin(n, origin, src, side):
        return pltpu.make_async_remote_copy(
            src_ref=src,
            dst_ref=shelf(n, origin, side),
            send_sem=twin_send.at[n, origin],
            recv_sem=twin_recv.at[n, origin],
            device_id={"member": chip * 2 + 1 - core},
            device_id_type=MESH,
        )

    def own_last(n):
        return pltpu.make_async_copy(last(n), shelf(n, chip, core), own_sem.at[n, 1])

    def has(step):
        return jnp.logical_and(chip + step >= 0, chip + step < chips)

    def launch(n):
        for step in (1, -1):

            @pl.when(has(step))
            def _():
                hop(n, chip, step, last(n)).start()

        twin(n, chip, last(n), core).start()
        own_last(n).start()
        start_all(n)

    gather(*cuts[0])
    pl.semaphore_wait(barrier, members - 1)
    launch(0)
    gather(*cuts[1])
    launch(1)
    for n in range(2):
        for far in range(1, chips):
            for step in (1, -1):
                origin = chip - step * far

                @pl.when(has(-step * far))
                def _():
                    held = shelf(n, origin, core)
                    hop(n, origin, step, held).wait_recv()
                    twin(n, origin, held, core).start()

                    @pl.when(has(step))
                    def _():
                        hop(n, origin, step, held).start()

    for n in range(2):
        own_last(n).wait()
        twin(n, chip, last(n), core).wait_send()
        twin(n, chip, last(n), 1 - core).wait_recv()
        for step in (1, -1):

            @pl.when(has(step))
            def _():
                hop(n, chip, step, last(n)).wait_send()

        for far in range(1, chips):
            for step in (1, -1):
                origin = chip - step * far

                @pl.when(has(-step * far))
                def _():
                    held = shelf(n, origin, core)
                    twin(n, origin, held, core).wait_send()
                    twin(n, origin, held, 1 - core).wait_recv()

                    @pl.when(has(step))
                    def _():
                        hop(n, origin, step, held).wait_send()

        finish_all(n)
    blank.wait()


def exchange(pick, a_rows, p_rows, members, slots, spill, total):
    size, step_lanes = a_rows.shape[0], p_rows.shape[0]
    dma = pltpu.SemaphoreType.DMA
    width = size + step_lanes
    sems = [dma((2, members)), dma((2, members)), dma((2, 2))]
    if spill:
        chips = members // 2
        sems += [dma((2, chips, 2)), dma((2, chips)), dma((2, chips)), dma((2, chips))]
    return pl.pallas_call(
        functools.partial(exchange_kernel, members, slots, spill, step_lanes),
        out_shape=jax.ShapeDtypeStruct((total, width), a_rows.dtype),
        in_specs=[pl.BlockSpec(memory_space=pltpu.VMEM)] * 3,
        out_specs=pl.BlockSpec(memory_space=pl.ANY),
        scratch_shapes=[
            pltpu.VMEM((pick.shape[0], width), a_rows.dtype),
            pltpu.VMEM((16, width), a_rows.dtype),
            dma,
        ]
        + sems,
        compiler_params=pltpu.CompilerParams(
            collective_id=1 if spill else 0,
            has_side_effects=True,
            vmem_limit_bytes=44 * 1024 * 1024,
        ),
        name="exchange_spill" if spill else "exchange_rows",
    )(pick, a_rows, p_rows)


def counts_kernel(groups, members, own_ref, all_ref, send_sem, recv_sem):
    devices = groups * members
    flat = lax.axis_index("group") * members + lax.axis_index("member")
    barrier = pltpu.get_barrier_semaphore()

    def target(o):
        other = lax.rem(flat + o, devices)
        return {"group": other // members, "member": lax.rem(other, members)}

    def greet(o, carry):
        pl.semaphore_signal(barrier, inc=1, device_id=target(o), device_id_type=MESH)
        return carry

    lax.fori_loop(1, devices, greet, 0)
    pl.semaphore_wait(barrier, devices - 1)

    def copy(o):
        return pltpu.make_async_remote_copy(
            src_ref=own_ref,
            dst_ref=all_ref.at[flat],
            send_sem=send_sem.at[o],
            recv_sem=recv_sem.at[o],
            device_id=target(o),
            device_id_type=MESH,
        )

    def start(o, carry):
        copy(o).start()
        return carry

    def finish(o, carry):
        copy(o).wait()
        return carry

    lax.fori_loop(1, devices, start, 0)
    all_ref[flat] = own_ref[...]
    lax.fori_loop(1, devices, finish, 0)


def share_counts(counts, groups, members):
    devices = groups * members
    own = jnp.pad(counts, (0, LANES - members))[None, :]
    return pl.pallas_call(
        functools.partial(counts_kernel, groups, members),
        out_shape=jax.ShapeDtypeStruct((devices, 1, LANES), counts.dtype),
        in_specs=[pl.BlockSpec(memory_space=pltpu.VMEM)],
        out_specs=pl.BlockSpec(memory_space=pltpu.VMEM),
        scratch_shapes=[pltpu.SemaphoreType.DMA((devices,))] * 2,
        compiler_params=pltpu.CompilerParams(collective_id=2, has_side_effects=True),
        name="share_counts",
    )(own)[:, 0, :members]


def shifted(x, k):
    width = x.shape[-1]
    if k == 0:
        return pltpu.roll(x, 1, axis=x.ndim - 1)
    if k == 2:
        return pltpu.roll(x, width - 1, axis=x.ndim - 1)
    return x


def setup_kernel(ext_ref, s_ref, co_ref, p3, s3, ap3, dinv, tiles, wide):
    _, modes, tile, rows = s_ref.shape
    width = ext_ref.shape[1]
    f32 = jnp.float32
    half = tile // 2
    parts = [(i, l) for l in range(width // LANES) for i in range(2)]
    line = lax.broadcasted_iota(jnp.int32, (tile, width), 0)

    def pick_diag(j, total):
        at = pl.multiple_of((tile + j) * tile, tile)
        return total + jnp.where(line == j, ext_ref[pl.ds(at, tile), :].astype(f32), 0.0)

    diag = lax.fori_loop(0, tile, pick_diag, jnp.zeros((tile, width), f32))
    dinv[...] = jnp.where(diag > 1.0, 1.0 / jnp.where(diag > 1.0, diag, 1.0), 0.0)
    for c in range(modes):
        own = ext_ref[pl.ds((3 * tile + c) * tile, tile), :].astype(f32)
        for k in range(3):
            p3[k, c] = shifted(own, k)

    def product(ks, rows, i0, l0):
        lanes = pl.ds(l0, LANES)

        def body(j8, accs):
            accs = list(accs)
            j0 = pl.multiple_of(j8 * 8, 8)
            for k in ks:
                vecs = [ref[pl.ds(j0, 8), lanes] for ref in rows(k)]
                for jj in range(8):
                    at = pl.multiple_of((k * tile + j0 + jj) * tile + i0, half)
                    a = ext_ref[pl.ds(at, half), lanes].astype(f32)
                    for c in range(modes):
                        accs[c] = accs[c] + a * vecs[c][jj : jj + 1]
            return tuple(accs)

        zero = jnp.zeros((half, LANES), f32)
        return lax.fori_loop(0, tile // 8, body, (zero,) * modes, unroll=2)

    def each_part(fn):
        def body(q, carry):
            fn(
                pl.multiple_of((q % 2) * half, half),
                pl.multiple_of((q // 2) * LANES, LANES),
            )
            return carry

        lax.fori_loop(0, len(parts), body, 0)

    for k in range(3):

        def smooth(i0, l0, k=k):
            accs = product([k], lambda k: [p3.at[k, c] for c in range(modes)], i0, l0)
            inv = 0.6 * dinv[pl.ds(i0, half), pl.ds(l0, LANES)]
            for c in range(modes):
                value = -inv * accs[c]
                if k == 1:
                    value = p3[1, c, pl.ds(i0, half), pl.ds(l0, LANES)] + value
                value = value.astype(jnp.bfloat16)
                s3[1, k, c, pl.ds(i0, half), pl.ds(l0, LANES)] = value.astype(f32)

        each_part(smooth)

    def spread_s(q, carry):
        t, c = q // modes, q % modes
        own = s3[1, t, c]
        s_ref[t, c] = pltpu.roll(own, width - HALO, axis=1)[:, :rows].astype(jnp.bfloat16)
        s3[0, t, c] = shifted(own, 0)
        s3[2, t, c] = shifted(own, 2)
        return carry

    lax.fori_loop(0, 3 * modes, spread_s, 0)

    for e in range(5):

        def prod(i0, l0, e=e):
            ks = [k for k in range(3) if 0 <= e - k <= 2]
            accs = product(ks, lambda k: [s3.at[k, e - k, c] for c in range(modes)], i0, l0)
            for c in range(modes):
                ap3[1, e, c, pl.ds(i0, half), pl.ds(l0, LANES)] = (
                    accs[c].astype(jnp.bfloat16).astype(f32)
                )

        each_part(prod)

    def spread_ap(q, carry):
        e, c = q // modes, q % modes
        own = ap3[1, e, c]
        ap3[0, e, c] = shifted(own, 0)
        ap3[2, e, c] = shifted(own, 2)
        return carry

    lax.fori_loop(0, 5 * modes, spread_ap, 0)

    for f in range(7):

        def coarse(q, carry, f=f):
            c, l0 = q // (width // LANES), pl.multiple_of((q % (width // LANES)) * LANES, LANES)
            lanes = pl.ds(l0, LANES)
            sums = [None] * modes
            for dn in (-1, 0, 1):
                e = f - 1 - dn
                if not 0 <= e <= 4:
                    continue
                s = s3[dn + 1, 1 - dn, c, :, lanes]
                for d in range(modes):
                    term = s * ap3[dn + 1, e, d, :, lanes]
                    term = jnp.sum(term.reshape(tile // 8, 8, LANES), axis=0)
                    sums[d] = term if sums[d] is None else sums[d] + term
            for d in range(modes):
                tiles[f, c, d : d + 1, lanes] = jnp.sum(sums[d], axis=0, keepdims=True)
            return carry

        lax.fori_loop(0, modes * (width // LANES), coarse, 0)

    count = 7 * modes * modes
    for f in range(7):
        for c in range(modes):
            at = (f * modes + c) * modes
            wide[at : at + modes, :] = tiles[f, c]
    wide[count:] = jnp.zeros((wide.shape[0] - count, width), f32)
    co_ref[...] = jnp.transpose(pltpu.roll(wide[...], width - HALO, axis=1))[:rows, :count]


def setup(ext, modes, tile, rows):
    width = ext.shape[1]
    count = 7 * modes * modes
    f32 = jnp.float32
    return pl.pallas_call(
        setup_kernel,
        out_shape=(
            jax.ShapeDtypeStruct((3, modes, tile, rows), jnp.bfloat16),
            jax.ShapeDtypeStruct((rows, count), f32),
        ),
        in_specs=[pl.BlockSpec(memory_space=pltpu.VMEM)],
        out_specs=(pl.BlockSpec(memory_space=pltpu.VMEM),) * 2,
        scratch_shapes=[
            pltpu.VMEM((3, modes, tile, width), f32),
            pltpu.VMEM((3, 3, modes, tile, width), f32),
            pltpu.VMEM((3, 5, modes, tile, width), f32),
            pltpu.VMEM((tile, width), f32),
            pltpu.VMEM((7, modes, modes, width), f32),
            pltpu.VMEM((-(-count // LANES) * LANES, width), f32),
        ],
        compiler_params=pltpu.CompilerParams(vmem_limit_bytes=28 * 1024 * 1024),
        name="coarse_setup",
    )(ext)


def per_device(a_band, p_tent, new_owner):
    members = lax.axis_size("member")
    groups = lax.axis_size("group")
    me = lax.axis_index("member")
    rows, _, tile, _ = a_band.shape
    modes = p_tent.shape[1]
    cap = 2 * rows // members
    slots = -(-cap // 16) * 16
    bf16, i32 = jnp.bfloat16, jnp.int32
    size = 3 * tile * tile
    width = -(-(rows + 2 * HALO) // LANES) * LANES
    spill = 16 if slots > 32 and members % 2 == 0 else 0
    few = slots - spill
    total = max(members * slots, members * (few + spill))

    onehot = (new_owner[None, :] == jnp.arange(members, dtype=i32)[:, None]).astype(i32)
    earlier = (jnp.arange(rows)[:, None] < jnp.arange(rows)[None, :]).astype(jnp.float32)
    before = jnp.dot(onehot.astype(jnp.float32), earlier).astype(i32)
    place = jnp.sum(before * onehot, 0)
    counts = jnp.sum(onehot, 1)
    axes = ("group", "member")
    if spill:
        every = share_counts(counts, groups, members)
        table = lax.dynamic_slice_in_dim(every, lax.axis_index("group") * members, members, 0)
    else:
        table = lax.all_gather(counts, "member")
    got = lax.dynamic_index_in_dim(table, me, 1, keepdims=False)

    a_rows = a_band.transpose(1, 3, 2, 0).reshape(size, rows)
    p_rows = p_tent.transpose(1, 2, 0).reshape(modes * tile, rows)
    member = jnp.arange(members)
    upto = member[None, :] <= member[:, None]
    starts = jnp.sum(jnp.where(upto, got[None, :], 0), 1) - got

    def picked(flat_slot, count):
        return (jnp.arange(count, dtype=i32)[:, None] == flat_slot[None, :]).astype(bf16)

    flat_slot = new_owner * slots + place

    def direct(own_a, own_p):
        pick = picked(flat_slot, members * slots)
        return exchange(pick, own_a, own_p, members, slots, 0, total + 16)

    def direct_lands():
        within = jnp.arange(slots, dtype=i32)
        lands = jnp.where(within[None, :] < got[:, None], starts[:, None] + within[None, :], -width)
        return jnp.pad(lands.reshape(-1), (0, total - members * slots), constant_values=-width)

    if spill:
        over = jnp.maximum(every - few, 0)
        fits = jnp.max(jnp.sum(over, 1)) <= spill

        mine = jnp.maximum(counts - few, 0)
        first = jnp.sum(jnp.where(upto, mine[None, :], 0), 1) - mine
        base = jnp.sum(first[:, None] * onehot, 0)
        spill_slot = jnp.where(
            place < few, new_owner * few + place, members * few + base + place - few
        )

        def spilled(own_a, own_p):
            pick = picked(spill_slot, members * few + spill)
            return exchange(pick, own_a, own_p, members, few, spill, total + 16)

        def spilled_lands():
            within = jnp.arange(few, dtype=i32)
            head = jnp.where(
                within[None, :] < got[:, None], starts[:, None] + within[None, :], -width
            )
            over_group = jnp.maximum(table - few, 0)
            before_me = jnp.sum(jnp.where(member[None, :] < me, over_group, 0), 1)
            at = jnp.arange(spill, dtype=i32)[None, :] - before_me[:, None]
            good = jnp.logical_and(at >= 0, at < jnp.maximum(got - few, 0)[:, None])
            tail = jnp.where(good, starts[:, None] + few + at, -width)
            lands = jnp.concatenate([head.reshape(-1), tail.reshape(-1)])
            return jnp.pad(lands, (0, total - members * (few + spill)), constant_values=-width)

        lands = jnp.where(fits, spilled_lands(), direct_lands())
        recv = lax.cond(fits, spilled, direct, a_rows, p_rows)
    else:
        lands = direct_lands()
        recv = direct(a_rows, p_rows)

    edge = jnp.arange(16, dtype=i32)
    edge_row = jnp.where(edge < HALO, edge, jnp.where(edge < 2 * HALO, rows - 2 * HALO + edge, -1))
    filled = jnp.concatenate([lands, jnp.full((16,), -width, i32)])
    rim_pick = (edge_row[:, None] == filled[None, :]).astype(bf16)
    rim = jnp.dot(rim_pick, recv, preferred_element_type=jnp.float32).astype(bf16)
    devices = groups * members
    up = [(i, i + 1) for i in range(devices - 1)]
    down = [(i + 1, i) for i in range(devices - 1)]
    from_left = lax.ppermute(rim[HALO : 2 * HALO], axes, up)
    from_right = lax.ppermute(rim[:HALO], axes, down)
    halo = jnp.concatenate(
        [from_left, from_right, jnp.zeros((16 - 2 * HALO, rim.shape[1]), bf16)], 0
    )
    recv = lax.dynamic_update_slice(recv, halo, (total, 0))
    halo_lane = jnp.where(edge < HALO, edge, jnp.where(edge < 2 * HALO, rows + edge, -1))
    lane = jnp.concatenate([lands + HALO, halo_lane])
    place_out = (lane[:, None] == jnp.arange(width, dtype=i32)[None, :]).astype(bf16)
    ext = lax.dot_general(
        recv, place_out, (((0,), (0,)), ((), ())), preferred_element_type=jnp.float32
    ).astype(bf16)
    s_out, coarse = setup(ext, modes, tile, rows)
    return (s_out.transpose(3, 0, 1, 2), coarse)


def solution(mesh):
    in_specs = (
        P(("group", "member"), None, None, None),
        P(("group", "member"), None, None),
        P(("group", "member")),
    )
    out_specs = (P(("group", "member"), None, None, None), P(("group", "member"), None))
    return jax.shard_map(
        per_device, mesh=mesh, in_specs=in_specs, out_specs=out_specs, check_vma=False
    )
```
